32 devices in a mesh: rve: 8 (over z, core), slab: 4 (over y, x).
Axes of the slice: x: 2, y: 2, z: 4, core: 2. Of those that a mesh axis runs over, the one named last changes fastest.
Arguments:
- phase_ids: int32 [64, 4096], P('slab'), may hold values from 0 to 1, as said below
- yield_flags: int32 [8, 3, 64, 4096], P('rve', None, 'slab'), may hold values from 0 to 1
- plastic_strain: float32 [8, 6, 64, 4096], P('rve', None, 'slab'), may hold values from -0.03 to 0.03
- displacements: float32 [8, 3], replicated, may hold values from -0.06 to 0.06
- connectivity: int32 [1, 8], replicated, may hold values from 0 to 7, as said below
Outputs:
- gauss_stress: float32 [8, 6], P('rve')
- gauss_tangent: float32 [8, 6, 6], P('rve')
- nodal_forces: float32 [8, 3], replicated
- stiffness: float32 [24, 24], replicated
The draws below stay inside these ranges and needn't reach their ends.
Inputs may be any that keep to these rules, and one draw needn't show every extreme that they name: `phase_ids`: 0 marks ferrite, 1 martensite. `connectivity`: element e is the cube [e, e+1] x [0,1] x [0,1]; entry c of its row is the id of its corner (e + c % 2, c // 2 % 2, c // 4); each point of the mesh has one id, distinct points distinct ids.
All inputs are finite; a program needn't handle non-finite values.
Results may differ from the reference program's by a relative error of at most 0.0001.
Values sent between devices are 32-bit elements; how exact they have to be, the bound alone decides.
A program may use at most 128 MiB of HBM per device.

```python
import math
import jax
import jax.numpy as jnp
import numpy as np
from jax import lax

GRID = 64
ITERS = 2
POINTS = 8
ELEMENTS = 1
NODES = 8


def phase_field(key):
    start_share = jax.random.randint(jax.random.fold_in(key, 11), (), 0, 500)
    finish_share = jax.random.randint(jax.random.fold_in(key, 13), (), 500, 1000)
    planes = lax.broadcasted_iota(jnp.int32, (GRID, GRID * GRID), 0)
    yield_limit = start_share + (finish_share - start_share) * planes // (GRID - 1)
    scores = jax.random.randint(jax.random.fold_in(key, 17), (GRID, GRID * GRID), 0, 1000)
    return (scores < yield_limit).astype(jnp.int32)


def draw_phase_ids(key, part):
    return phase_field(key)


def draw_yield_flags(key, part):
    phases = phase_field(key)
    soft_share = jax.random.randint(jax.random.fold_in(key, 31), (POINTS, ITERS + 1, 1, 1), 400, 1000)
    hard_share = jax.random.randint(jax.random.fold_in(key, 37), (POINTS, ITERS + 1, 1, 1), 0, 400)
    scores = jax.random.randint(jax.random.fold_in(key, 43), (POINTS, ITERS + 1, GRID, GRID * GRID), 0, 1000)
    yield_limit = jnp.where(phases[None, None] == 1, hard_share, soft_share)
    return (scores < yield_limit).astype(jnp.int32)


def draw_plastic_strain(key, part):
    offsets = jnp.clip(0.005 * jax.random.normal(jax.random.fold_in(key, 53), (POINTS, 6, 1, 1), jnp.float32), -0.015, 0.015)
    rough_part = jnp.clip(0.003 * jax.random.normal(jax.random.fold_in(key, 61), (POINTS, 6, GRID, GRID * GRID), jnp.float32), -0.012, 0.012)
    return (offsets + rough_part).astype(jnp.float32)


def draw_connectivity(key, part):
    ordering = jax.random.permutation(jax.random.fold_in(key, 71), NODES).astype(jnp.int32)
    element_index = lax.broadcasted_iota(jnp.int32, (ELEMENTS, 8), 0)
    corner_index = lax.broadcasted_iota(jnp.int32, (ELEMENTS, 8), 1)
    structured = (element_index + corner_index % 2) * 4 + corner_index // 2 % 2 * 2 + corner_index // 4
    return ordering[structured].astype(jnp.int32)


def noise(stream_key, dims, spread, limit, kind=jnp.bfloat16):
    values = jax.random.normal(stream_key, dims, jnp.float32) * spread
    return jnp.minimum(jnp.maximum(values, -limit), limit).astype(kind)


def setup_inputs(seed: int = 0) -> dict:
    keys = jax.random.split(jax.random.key(seed), 6)
    return {
        "phase_ids": draw_phase_ids(jax.random.fold_in(keys[5], 71), 0),
        "yield_flags": draw_yield_flags(jax.random.fold_in(keys[5], 71), 0),
        "plastic_strain": draw_plastic_strain(jax.random.fold_in(keys[5], 71), 0),
        "displacements": noise(keys[3], (NODES, 3), 0.01, 0.06, jnp.float32),
        "connectivity": draw_connectivity(jax.random.fold_in(keys[5], 71), 0),
    }


SHEAR_MODULUS = 80.0
BULK_MODULUS = 160.0
REFERENCE_SHEAR = 80.0
REFERENCE_LAME = 160.0 - 160.0 / 3.0
TANGENT_UNIT = 100.0
QUADRATURE_WEIGHT = 0.125
DIAGONAL_PART = (1.0, 1.0, 1.0, 0.0, 0.0, 0.0)
PAIR_WEIGHTS = (1.0, 1.0, 1.0, 2.0, 2.0, 2.0)
TENSOR_PAIRS = ((0, 0), (1, 1), (2, 2), (1, 2), (0, 2), (0, 1))
TENSOR_ROWS = ((0, 5, 4), (5, 1, 3), (4, 3, 2))

def gradient_table():
    inverse_root = 1.0 / math.sqrt(3.0)
    table_rows = np.zeros((8, 6, 24))
    for gauss_corner in range(8):
        position = [0.5 + (2 * (gauss_corner >> axis_number & 1) - 1) * 0.5 * inverse_root for axis_number in range(3)]
        for corner in range(8):
            corner_bits = [corner >> axis_number & 1 for axis_number in range(3)]
            factors = [position[axis_number] * corner_bits[axis_number] + (1.0 - position[axis_number]) * (1 - corner_bits[axis_number]) for axis_number in range(3)]
            slopes = []
            for axis_number in range(3):
                slope_value = 2.0 * corner_bits[axis_number] - 1.0
                for other_axis in range(3):
                    if other_axis != axis_number:
                        slope_value = slope_value * factors[other_axis]
                slopes.append(slope_value)
            column = 3 * corner
            table_rows[gauss_corner, 0, column] += slopes[0]
            table_rows[gauss_corner, 1, column + 1] += slopes[1]
            table_rows[gauss_corner, 2, column + 2] += slopes[2]
            table_rows[gauss_corner, 3, column + 1] += 0.5 * slopes[2]
            table_rows[gauss_corner, 3, column + 2] += 0.5 * slopes[1]
            table_rows[gauss_corner, 4, column] += 0.5 * slopes[2]
            table_rows[gauss_corner, 4, column + 2] += 0.5 * slopes[0]
            table_rows[gauss_corner, 5, column] += 0.5 * slopes[1]
            table_rows[gauss_corner, 5, column + 1] += 0.5 * slopes[0]
    return table_rows

def point_geometry(points, connectivity, corner_lookup, node_count):
    element_count = connectivity.shape[0]
    point_count = points.shape[0]
    corner_selector = (points[:, None] % 8 == jnp.arange(8, dtype=jnp.int32)[None, :]).astype(jnp.float32)
    strain_row_values = jnp.einsum('zu,utf->ztf', corner_selector, corner_lookup, precision=lax.Precision.HIGHEST)
    element_onehot = points[:, None] // 8 == jnp.arange(element_count, dtype=jnp.int32)[None, :]
    corner_nodes = lax.optimization_barrier(jnp.sum(jnp.where(element_onehot[:, :, None], connectivity[None, :, :], 0), axis=1)).astype(jnp.int32)
    degrees = 3 * corner_nodes[:, :, None] + jnp.arange(3, dtype=jnp.int32)[None, None, :]
    degrees = degrees.reshape(point_count, 24)
    placing = (degrees[:, :, None] == jnp.arange(3 * node_count, dtype=jnp.int32)[None, None, :]).astype(jnp.float32)
    return (strain_row_values, placing)

def macro_strains(strain_row_values, placing, displacements):
    nodal_quantities = jnp.einsum('gpn,n->gp', placing, displacements.reshape(-1), precision=lax.Precision.HIGHEST)
    return jnp.einsum('vxw,vw->vx', strain_row_values, nodal_quantities, precision=lax.Precision.HIGHEST)

def material_response(strain, plastic, phase_ids, flag_values):
    diagonal = jnp.asarray(DIAGONAL_PART, jnp.float32)[:, None]
    weights = jnp.asarray(PAIR_WEIGHTS, jnp.float32)[:, None]
    martensite = phase_ids == 1
    yield_stress = jnp.where(martensite, 1.2, 0.3).astype(jnp.float32)
    hardening = jnp.where(martensite, 10.0, 2.0).astype(jnp.float32)
    elastic = strain - plastic
    volume = elastic[0] + elastic[1] + elastic[2]
    trial_dev = 2.0 * SHEAR_MODULUS * (elastic - diagonal * (volume / 3.0))
    equivalent = jnp.sqrt(1.5 * lax.optimization_barrier(jnp.sum(weights * trial_dev * trial_dev, axis=0)))
    bounded = jnp.maximum(equivalent, yield_stress)
    return_ratio = 3.0 * SHEAR_MODULUS / (3.0 * SHEAR_MODULUS + hardening)
    active = flag_values.astype(jnp.float32)
    plastic_flow = active * (equivalent - yield_stress) / bounded
    softening = 1.0 - return_ratio * plastic_flow
    stress = trial_dev * softening + diagonal * (BULK_MODULUS * volume)
    shear_term = 2.0 * SHEAR_MODULUS * softening
    tangent_weight = 3.0 * SHEAR_MODULUS * return_ratio * active * yield_stress / (bounded * bounded * bounded)
    return (stress, trial_dev, shear_term, tangent_weight)

def wave_terms(index_x, index_y, index_z):
    middle = GRID // 2
    signed = []
    for indices in (index_x, index_y, index_z):
        wrapped = jnp.where(indices < middle, indices, indices - GRID)
        signed.append(jnp.where(indices == middle, 0, wrapped))
    nyquist_free = (index_x != middle) & (index_y != middle) & (index_z != middle)
    length = signed[0] * signed[0] + signed[1] * signed[1] + signed[2] * signed[2]
    keep_mask = (nyquist_free & (length > 0)).astype(jnp.float32)
    inverse_length = 1.0 / jnp.sqrt(jnp.maximum(length, 1).astype(jnp.float32))
    normals = [signed_entry.astype(jnp.float32) * inverse_length for signed_entry in signed]
    return (normals, keep_mask)

def project_green(components, normals, keep_mask):
    traction = [components[tensor_row[0]] * normals[0] + components[tensor_row[1]] * normals[1] + components[tensor_row[2]] * normals[2] for tensor_row in TENSOR_ROWS]
    normal_load = normals[0] * traction[0] + normals[1] * traction[1] + normals[2] * traction[2]
    coupling = (REFERENCE_LAME + REFERENCE_SHEAR) / (REFERENCE_SHEAR * (REFERENCE_LAME + 2.0 * REFERENCE_SHEAR))
    result_list = []
    for left_axis, right_axis in TENSOR_PAIRS:
        entry_value = (normals[left_axis] * traction[right_axis] + normals[right_axis] * traction[left_axis]) / (2.0 * REFERENCE_SHEAR)
        entry_value = entry_value - coupling * normals[left_axis] * normals[right_axis] * normal_load
        result_list.append(entry_value * keep_mask)
    return jnp.stack(result_list)

def tangent_matrix(mean_shear, outer_sum):
    diagonal = jnp.asarray(DIAGONAL_PART, jnp.float32)
    volumetric = diagonal[:, None] * diagonal[None, :]
    weights = jnp.asarray(PAIR_WEIGHTS, jnp.float32)
    identity = jnp.eye(6, dtype=jnp.float32)
    whole = BULK_MODULUS * volumetric + mean_shear * (identity - volumetric / 3.0) - outer_sum * weights[None, :]
    return whole / TANGENT_UNIT

def assemble(stress_values, tangent_moduli, strain_row_values, placing):
    weights = jnp.asarray(PAIR_WEIGHTS, jnp.float32)
    force_row_values = strain_row_values * weights[None, :, None]
    element_force_vector = QUADRATURE_WEIGHT * jnp.einsum('mbh,mb->mh', force_row_values, stress_values, precision=lax.Precision.HIGHEST)
    element_stiffness_matrix = QUADRATURE_WEIGHT * jnp.einsum('xoh,xon,xnv->xhv', force_row_values, tangent_moduli, strain_row_values, precision=lax.Precision.HIGHEST)
    forces = jnp.einsum('gp,gpn->n', element_force_vector, placing, precision=lax.Precision.HIGHEST)
    stiffness = jnp.einsum('gpq,gpm,gqn->mn', element_stiffness_matrix, placing, placing, precision=lax.Precision.HIGHEST)
    return (forces.reshape(-1, 3), stiffness)

def reference(phase_ids, yield_flags, plastic_strain, displacements, connectivity):
    corner_lookup = jnp.asarray(gradient_table(), jnp.float32)
    points = jnp.arange(POINTS, dtype=jnp.int32)
    strain_row_values, placing = point_geometry(points, connectivity, corner_lookup, displacements.shape[0])
    macro_all = macro_strains(strain_row_values, placing, displacements)
    index_x = lax.broadcasted_iota(jnp.int32, (GRID, 1, 1), 0)
    index_y = lax.broadcasted_iota(jnp.int32, (1, GRID, 1), 1)
    index_z = lax.broadcasted_iota(jnp.int32, (1, 1, GRID), 2)
    normals, keep_mask = wave_terms(index_x, index_y, index_z)
    phases = phase_ids.reshape(-1)
    voxel_count = float(GRID ** 3)

    def one_point(inputs):
        macro_strain, plastic_cell, point_flags = inputs
        plastic = plastic_cell.reshape(6, -1)
        strain = jnp.broadcast_to(macro_strain[:, None], plastic.shape)
        for iteration in range(ITERS):
            stress = material_response(strain, plastic, phases, point_flags[iteration].reshape(-1))[0]
            spectrum = jnp.fft.fftn(stress.reshape(6, GRID, GRID, GRID), axes=(1, 2, 3))
            corrected = project_green([spectrum[component] for component in range(6)], normals, keep_mask)
            strain = strain - jnp.real(jnp.fft.ifftn(corrected, axes=(1, 2, 3))).reshape(6, -1)
        stress, trial_dev, shear_term, tangent_weight = material_response(strain, plastic, phases, point_flags[ITERS].reshape(-1))
        mean_stress = lax.optimization_barrier(jnp.sum(stress, axis=1)) / voxel_count
        mean_shear = jnp.sum(shear_term) / voxel_count
        outer_sum = jnp.dot(trial_dev * tangent_weight[None, :], trial_dev.T, precision=lax.Precision.HIGHEST) / voxel_count
        return (mean_stress, tangent_matrix(mean_shear, outer_sum))
    stress_values, tangent_moduli = lax.map(one_point, (macro_all, plastic_strain, yield_flags))
    forces, stiffness = assemble(stress_values, tangent_moduli, strain_row_values, placing)
    return (stress_values, tangent_moduli, forces, stiffness)
```

```python
import math

import jax
import jax.numpy as jnp
import numpy as np
from jax import lax
from jax.experimental import pallas as pl
from jax.experimental.pallas import tpu as pltpu
from jax.sharding import PartitionSpec as P

GRID = 64
ITERS = 2


SHEAR_MODULUS = 80.0
BULK_MODULUS = 160.0
REFERENCE_SHEAR = 80.0
REFERENCE_LAME = 160.0 - 160.0 / 3.0
TANGENT_UNIT = 100.0
QUADRATURE_WEIGHT = 0.125
DIAGONAL_PART = (1.0, 1.0, 1.0, 0.0, 0.0, 0.0)
PAIR_WEIGHTS = (1.0, 1.0, 1.0, 2.0, 2.0, 2.0)
TENSOR_PAIRS = ((0, 0), (1, 1), (2, 2), (1, 2), (0, 2), (0, 1))
TENSOR_ROWS = ((0, 5, 4), (5, 1, 3), (4, 3, 2))


def gradient_table():
    inverse_root = 1.0 / math.sqrt(3.0)
    table_rows = np.zeros((8, 6, 24))
    for gauss_corner in range(8):
        position = [
            0.5 + (2 * (gauss_corner >> axis_number & 1) - 1) * 0.5 * inverse_root
            for axis_number in range(3)
        ]
        for corner in range(8):
            corner_bits = [corner >> axis_number & 1 for axis_number in range(3)]
            factors = [
                position[axis_number] * corner_bits[axis_number]
                + (1.0 - position[axis_number]) * (1 - corner_bits[axis_number])
                for axis_number in range(3)
            ]
            slopes = []
            for axis_number in range(3):
                slope_value = 2.0 * corner_bits[axis_number] - 1.0
                for other_axis in range(3):
                    if other_axis != axis_number:
                        slope_value = slope_value * factors[other_axis]
                slopes.append(slope_value)
            column = 3 * corner
            table_rows[gauss_corner, 0, column] += slopes[0]
            table_rows[gauss_corner, 1, column + 1] += slopes[1]
            table_rows[gauss_corner, 2, column + 2] += slopes[2]
            table_rows[gauss_corner, 3, column + 1] += 0.5 * slopes[2]
            table_rows[gauss_corner, 3, column + 2] += 0.5 * slopes[1]
            table_rows[gauss_corner, 4, column] += 0.5 * slopes[2]
            table_rows[gauss_corner, 4, column + 2] += 0.5 * slopes[0]
            table_rows[gauss_corner, 5, column] += 0.5 * slopes[1]
            table_rows[gauss_corner, 5, column + 1] += 0.5 * slopes[0]
    return table_rows


def point_geometry(points, connectivity, corner_lookup, node_count):
    element_count = connectivity.shape[0]
    point_count = points.shape[0]
    corner_selector = (points[:, None] % 8 == jnp.arange(8, dtype=jnp.int32)[None, :]).astype(
        jnp.float32
    )
    strain_row_values = jnp.einsum(
        "zu,utf->ztf", corner_selector, corner_lookup, precision=lax.Precision.HIGHEST
    )
    element_onehot = points[:, None] // 8 == jnp.arange(element_count, dtype=jnp.int32)[None, :]
    corner_nodes = jnp.sum(
        jnp.where(element_onehot[:, :, None], connectivity[None, :, :], 0), axis=1
    )
    degrees = 3 * corner_nodes[:, :, None] + jnp.arange(3, dtype=jnp.int32)[None, None, :]
    degrees = degrees.reshape(point_count, 24)
    placing = (
        degrees[:, :, None] == jnp.arange(3 * node_count, dtype=jnp.int32)[None, None, :]
    ).astype(jnp.float32)
    return (strain_row_values, placing)


def macro_strains(strain_row_values, placing, displacements):
    nodal_quantities = jnp.einsum(
        "gpn,n->gp", placing, displacements.reshape(-1), precision=lax.Precision.HIGHEST
    )
    return jnp.einsum(
        "vxw,vw->vx", strain_row_values, nodal_quantities, precision=lax.Precision.HIGHEST
    )


def material_response(strain, plastic, phase_ids, flag_values):
    diagonal = jnp.asarray(DIAGONAL_PART, jnp.float32)[:, None]
    weights = jnp.asarray(PAIR_WEIGHTS, jnp.float32)[:, None]
    martensite = phase_ids == 1
    yield_stress = jnp.where(martensite, 1.2, 0.3).astype(jnp.float32)
    hardening = jnp.where(martensite, 10.0, 2.0).astype(jnp.float32)
    elastic = strain - plastic
    volume = elastic[0] + elastic[1] + elastic[2]
    trial_dev = 2.0 * SHEAR_MODULUS * (elastic - diagonal * (volume / 3.0))
    equivalent = jnp.sqrt(1.5 * jnp.sum(weights * trial_dev * trial_dev, axis=0))
    bounded = jnp.maximum(equivalent, yield_stress)
    return_ratio = 3.0 * SHEAR_MODULUS / (3.0 * SHEAR_MODULUS + hardening)
    active = flag_values.astype(jnp.float32)
    plastic_flow = active * (equivalent - yield_stress) / bounded
    softening = 1.0 - return_ratio * plastic_flow
    stress = trial_dev * softening + diagonal * (BULK_MODULUS * volume)
    shear_term = 2.0 * SHEAR_MODULUS * softening
    tangent_weight = (
        3.0 * SHEAR_MODULUS * return_ratio * active * yield_stress / (bounded * bounded * bounded)
    )
    return (stress, trial_dev, shear_term, tangent_weight)


def wave_terms(index_x, index_y, index_z):
    middle = GRID // 2
    signed = []
    for indices in (index_x, index_y, index_z):
        wrapped = jnp.where(indices < middle, indices, indices - GRID)
        signed.append(jnp.where(indices == middle, 0, wrapped))
    nyquist_free = (index_x != middle) & (index_y != middle) & (index_z != middle)
    length = signed[0] * signed[0] + signed[1] * signed[1] + signed[2] * signed[2]
    keep_mask = (nyquist_free & (length > 0)).astype(jnp.float32)
    inverse_length = 1.0 / jnp.sqrt(jnp.maximum(length, 1).astype(jnp.float32))
    normals = [signed_entry.astype(jnp.float32) * inverse_length for signed_entry in signed]
    return (normals, keep_mask)


def project_green(components, normals, keep_mask):
    traction = [
        components[tensor_row[0]] * normals[0]
        + components[tensor_row[1]] * normals[1]
        + components[tensor_row[2]] * normals[2]
        for tensor_row in TENSOR_ROWS
    ]
    normal_load = normals[0] * traction[0] + normals[1] * traction[1] + normals[2] * traction[2]
    coupling = (REFERENCE_LAME + REFERENCE_SHEAR) / (
        REFERENCE_SHEAR * (REFERENCE_LAME + 2.0 * REFERENCE_SHEAR)
    )
    result_list = []
    for left_axis, right_axis in TENSOR_PAIRS:
        entry_value = (
            normals[left_axis] * traction[right_axis] + normals[right_axis] * traction[left_axis]
        ) / (2.0 * REFERENCE_SHEAR)
        entry_value = (
            entry_value - coupling * normals[left_axis] * normals[right_axis] * normal_load
        )
        result_list.append(entry_value * keep_mask)
    return jnp.stack(result_list)


def tangent_matrix(mean_shear, outer_sum):
    diagonal = jnp.asarray(DIAGONAL_PART, jnp.float32)
    volumetric = diagonal[:, None] * diagonal[None, :]
    weights = jnp.asarray(PAIR_WEIGHTS, jnp.float32)
    identity = jnp.eye(6, dtype=jnp.float32)
    whole = (
        BULK_MODULUS * volumetric
        + mean_shear * (identity - volumetric / 3.0)
        - outer_sum * weights[None, :]
    )
    return whole / TANGENT_UNIT


def assemble(stress_values, tangent_moduli, strain_row_values, placing):
    weights = jnp.asarray(PAIR_WEIGHTS, jnp.float32)
    force_row_values = strain_row_values * weights[None, :, None]
    element_force_vector = QUADRATURE_WEIGHT * jnp.einsum(
        "mbh,mb->mh", force_row_values, stress_values, precision=lax.Precision.HIGHEST
    )
    element_stiffness_matrix = QUADRATURE_WEIGHT * jnp.einsum(
        "xoh,xon,xnv->xhv",
        force_row_values,
        tangent_moduli,
        strain_row_values,
        precision=lax.Precision.HIGHEST,
    )
    forces = jnp.einsum("gp,gpn->n", element_force_vector, placing, precision=lax.Precision.HIGHEST)
    stiffness = jnp.einsum(
        "gpq,gpm,gqn->mn",
        element_stiffness_matrix,
        placing,
        placing,
        precision=lax.Precision.HIGHEST,
    )
    return (forces.reshape(-1, 3), stiffness)


def angle_table(count_rows, count_cols):
    rows_index = lax.broadcasted_iota(jnp.int32, (count_rows, count_cols), 0)
    cols_index = lax.broadcasted_iota(jnp.int32, (count_rows, count_cols), 1)
    angles = 2.0 * math.pi / GRID * (rows_index * cols_index % GRID).astype(jnp.float32)
    return (jnp.cos(angles), jnp.sin(angles))


def complex_table(inverse):
    cosine, sine = angle_table(GRID, GRID)
    if inverse:
        first_row = jnp.stack([cosine, -sine], axis=1)
        second_row = jnp.stack([sine, cosine], axis=1)
    else:
        first_row = jnp.stack([cosine, sine], axis=1)
        second_row = jnp.stack([-sine, cosine], axis=1)
    return jnp.stack([first_row, second_row], axis=0)


def on_device(phase_ids, yield_flags, plastic_strain, displacements, connectivity):
    slabs = lax.axis_size("slab")
    slab_index = lax.axis_index("slab")
    plane_count = phase_ids.shape[0]
    row_planes = GRID // slabs
    node_count = displacements.shape[0]
    corner_lookup = jnp.asarray(gradient_table(), jnp.float32)
    gauss_point = lax.axis_index("rve")
    own_points = jnp.full((1,), gauss_point, jnp.int32)
    strain_row_values, placing = point_geometry(own_points, connectivity, corner_lookup, node_count)
    macro_strain = macro_strains(strain_row_values, placing, displacements)[0]
    phases = phase_ids.reshape(-1)
    plastic = plastic_strain[0].reshape(6, -1)
    point_flags = yield_flags[0]
    columns = GRID // 2
    kept_index = lax.broadcasted_iota(jnp.int32, (columns, 1), 0)
    column_weight = jnp.where(kept_index == 0, 1.0, 2.0).astype(jnp.float32)
    depth_cos, depth_sin = angle_table(columns, GRID)
    forward_depth = jnp.stack([depth_cos, -depth_sin], axis=0)
    inverse_depth = jnp.stack(
        [column_weight * depth_cos, -column_weight * depth_sin], axis=0
    ) / float(GRID**3)
    forward_plane = complex_table(False)
    inverse_plane = complex_table(True)
    index_x = lax.broadcasted_iota(jnp.int32, (GRID, 1, 1), 0)
    index_y = slab_index * row_planes + lax.broadcasted_iota(jnp.int32, (1, row_planes, 1), 1)
    index_z = lax.broadcasted_iota(jnp.int32, (1, 1, columns), 2)
    normals, keep_mask = wave_terms(index_x, index_y, index_z)
    strain = jnp.broadcast_to(macro_strain[:, None], plastic.shape)
    for iteration in range(ITERS):
        stress = material_response(strain, plastic, phases, point_flags[iteration].reshape(-1))[0]
        voxel_block = stress.reshape(6, plane_count, GRID, GRID)
        spectral = jnp.einsum(
            "pkz,cxyz->pcxyk", forward_depth, voxel_block, precision=lax.Precision.HIGHEST
        )
        spectral = jnp.einsum(
            "pjqy,qcxyk->pcxjk", forward_plane, spectral, precision=lax.Precision.HIGHEST
        )
        spectral = lax.all_to_all(spectral, "slab", split_axis=3, concat_axis=2, tiled=True)
        spectral = jnp.einsum(
            "pjqx,qcxyk->pcjyk", forward_plane, spectral, precision=lax.Precision.HIGHEST
        )
        projected = project_green(
            [spectral[:, component] for component in range(6)], normals, keep_mask
        )
        spectral = jnp.einsum(
            "pjqx,cqxyk->pcjyk", inverse_plane, projected, precision=lax.Precision.HIGHEST
        )
        spectral = lax.all_to_all(spectral, "slab", split_axis=2, concat_axis=3, tiled=True)
        spectral = jnp.einsum(
            "pjqy,qcxyk->pcxjk", inverse_plane, spectral, precision=lax.Precision.HIGHEST
        )
        correction = jnp.einsum(
            "pkz,pcxyk->cxyz", inverse_depth, spectral, precision=lax.Precision.HIGHEST
        )
        strain = strain - correction.reshape(6, -1)
    stress, trial_dev, shear_term, tangent_weight = material_response(
        strain, plastic, phases, point_flags[ITERS].reshape(-1)
    )
    outer_part = jnp.dot(
        trial_dev * tangent_weight[None, :], trial_dev.T, precision=lax.Precision.HIGHEST
    )
    stress_total, shear_total, outer_total = lax.psum(
        (jnp.sum(stress, axis=1), jnp.sum(shear_term), outer_part), "slab"
    )
    voxel_count = float(GRID**3)
    mean_stress = stress_total / voxel_count
    tangent = tangent_matrix(shear_total / voxel_count, outer_total / voxel_count)
    own_forces, own_stiffness = assemble(
        mean_stress[None], tangent[None], strain_row_values, placing
    )
    forces, stiffness = lax.psum((own_forces, own_stiffness), "rve")
    return (mean_stress[None], tangent[None], forces, stiffness)


ROUGH = 16
GROUPS = 4
LANES = 128
STATS = 32
MESH = pl.DeviceIdType.MESH


def halves(value):
    high = value.astype(jnp.bfloat16)
    return high, (value - high.astype(jnp.float32)).astype(jnp.bfloat16)


def mul(left, right):
    return jnp.dot(left, right, preferred_element_type=jnp.float32)


def host_halves(table):
    table = np.asarray(table, np.float32)
    high = table.astype(jnp.bfloat16)
    low = (table - high.astype(np.float32)).astype(jnp.bfloat16)
    return jnp.asarray(np.stack([high, low]))


def depth_tables():
    kept = GRID // 2
    angles = 2.0 * np.pi / GRID * (np.arange(GRID)[:, None] * np.arange(kept)[None, :] % GRID)
    weight = np.where(np.arange(kept) == 0, 1.0, 2.0) / float(GRID**3)
    eye = np.eye(GROUPS)
    forward = np.concatenate([np.kron(eye, np.cos(angles)), np.kron(eye, -np.sin(angles))], axis=1)
    back_cos = (np.cos(angles) * weight[None, :]).T
    back_sin = (-np.sin(angles) * weight[None, :]).T
    inverse = np.concatenate([np.kron(eye, back_cos), np.kron(eye, back_sin)], axis=0)
    return forward, inverse


def line_tables():
    angles = 2.0 * np.pi / GRID * (np.arange(GRID)[:, None] * np.arange(GRID)[None, :] % GRID)
    cosine, sine = np.cos(angles), np.sin(angles)
    forward = np.block([[cosine, sine], [-sine, cosine]])
    inverse = np.block([[cosine, -sine], [sine, cosine]])
    return forward, inverse


def twiddle_table():
    lane_group = np.arange(LANES) // (LANES // GROUPS)
    angles = 2.0 * np.pi / GRID * (np.arange(ROUGH)[:, None] * lane_group[None, :])
    return jnp.asarray(np.stack([np.cos(angles), -np.sin(angles)], axis=1), jnp.float32)


def four_point(re, im, sign):
    a_re, a_im = re[0] + re[2], im[0] + im[2]
    b_re, b_im = re[0] - re[2], im[0] - im[2]
    c_re, c_im = re[1] + re[3], im[1] + im[3]
    d_re, d_im = re[1] - re[3], im[1] - im[3]
    e_re, e_im = (d_im, -d_re) if sign < 0 else (-d_im, d_re)
    return (
        [a_re + c_re, b_re + e_re, a_re - c_re, b_re - e_re],
        [a_im + c_im, b_im + e_im, a_im - c_im, b_im - e_im],
    )


def sixteen_point(re, im, sign):
    inner_re, inner_im = [], []
    for b in range(4):
        part_re, part_im = four_point(re[b::4], im[b::4], sign)
        for ka in range(1, 4):
            if b:
                angle = 2.0 * math.pi * b * ka / 16.0
                cosine, sine = math.cos(angle), sign * math.sin(angle)
                old_re, old_im = part_re[ka], part_im[ka]
                part_re[ka] = old_re * cosine - old_im * sine
                part_im[ka] = old_re * sine + old_im * cosine
        inner_re.append(part_re)
        inner_im.append(part_im)
    out_re, out_im = [None] * 16, [None] * 16
    for ka in range(4):
        part_re, part_im = four_point(
            [inner_re[b][ka] for b in range(4)], [inner_im[b][ka] for b in range(4)], sign
        )
        for kb in range(4):
            out_re[ka + 4 * kb] = part_re[kb]
            out_im[ka + 4 * kb] = part_im[kb]
    return out_re, out_im


def voxel_law(elastic, phase, flag, want_tangent):
    martensite = phase == 1
    yield_stress = jnp.where(martensite, 1.2, 0.3).astype(jnp.float32)
    base = 3.0 * SHEAR_MODULUS
    ratio = jnp.where(martensite, base / (base + 10.0), base / (base + 2.0)).astype(jnp.float32)
    volume = elastic[0] + elastic[1] + elastic[2]
    third = volume * (1.0 / 3.0)
    trial = [
        (2.0 * SHEAR_MODULUS) * (elastic[n] - third if n < 3 else elastic[n]) for n in range(6)
    ]
    square = [value * value for value in trial]
    norm = square[0] + square[1] + square[2] + 2.0 * (square[3] + square[4] + square[5])
    equivalent = jnp.sqrt(1.5 * norm)
    bounded = jnp.maximum(equivalent, yield_stress)
    active = flag.astype(jnp.float32)
    inverse = 1.0 / bounded
    active_ratio = active * ratio
    softening = 1.0 - active_ratio * ((equivalent - yield_stress) * inverse)
    pressure = BULK_MODULUS * volume
    stress = [trial[n] * softening + pressure if n < 3 else trial[n] * softening for n in range(6)]
    if not want_tangent:
        return stress
    beta = base * active_ratio * yield_stress * (inverse * inverse * inverse)
    return stress, trial, (2.0 * SHEAR_MODULUS) * softening, beta


def cell_kernel(
    slabs, points, macro_ref, phase_ref, flag_ref, plastic_ref, depth_ref, depth_back_ref,
    line_ref, line_back_ref, twiddle_ref, out_ref,
    elastic, planes, lines, lines_back, planes_back, work, sums, slab_sums, point_sums,
    send_sem, recv_sem, slab_send, slab_recv, point_send, point_recv,
):
    slab = lax.axis_index("slab")
    point = lax.axis_index("rve")
    rows = GRID // slabs
    own_lines = ROUGH // slabs
    wide = GROUPS * GRID

    barrier = pltpu.get_barrier_semaphore()
    for step in range(1, slabs):
        pl.semaphore_signal(
            barrier, inc=1, device_id={"slab": lax.rem(slab + step, slabs)}, device_id_type=MESH
        )
    for step in range(1, points):
        pl.semaphore_signal(
            barrier, inc=1, device_id={"rve": lax.rem(point + step, points)}, device_id_type=MESH
        )

    def lane_block(index):
        return pl.ds(pl.multiple_of(index * wide, wide), wide)

    def row_block(index):
        return pl.ds(pl.multiple_of(index * rows, rows), rows)

    @pl.loop(0, ROUGH)
    def _(block):
        for n in range(6):
            elastic[n, :, lane_block(block)] = macro_ref[n] - plastic_ref[n, :, lane_block(block)]

    lane = lax.broadcasted_iota(jnp.int32, (1, LANES), 1)
    group = lane >> 5
    high_sign = jnp.where((group >> 1) == 0, 1.0, -1.0).astype(jnp.float32)
    low_sign = jnp.where((group & 1) == 0, 1.0, -1.0).astype(jnp.float32)
    low_first = (group & 1) == 0
    corner = group == 3

    def across_high(value):
        return pltpu.roll(value, 64, 1) + high_sign * value

    def across_low(value):
        partner = jnp.where(low_first, pltpu.roll(value, 96, 1), pltpu.roll(value, 32, 1))
        return partner + low_sign * value

    def groups_forward(re, im, cosine, sine):
        re, im = re * cosine - im * sine, re * sine + im * cosine
        re, im = across_high(re), across_high(im)
        re, im = jnp.where(corner, im, re), jnp.where(corner, -re, im)
        return across_low(re), across_low(im)

    def groups_back(re, im, cosine, sine):
        re, im = across_low(re), across_low(im)
        re, im = jnp.where(corner, -im, re), jnp.where(corner, re, im)
        re, im = across_high(re), across_high(im)
        return re * cosine + im * sine, im * cosine - re * sine

    def sixteen(ref, sign):
        @pl.loop(0, 6)
        def _(n):
            for half in range(rows // 8):
                part = pl.ds(half * 8, 8)
                re = [ref[n, 0, k, part, :] for k in range(ROUGH)]
                im = [ref[n, 1, k, part, :] for k in range(ROUGH)]
                re, im = sixteen_point(re, im, sign)
                for k in range(ROUGH):
                    ref[n, 0, k, part, :] = re[k]
                    ref[n, 1, k, part, :] = im[k]

    def forward_copy(step, chunk, target, source):
        return pltpu.make_async_remote_copy(
            src_ref=planes.at[:, :, target * own_lines + chunk],
            dst_ref=lines.at[:, :, chunk, row_block(source), :],
            send_sem=send_sem.at[0, step - 1, chunk],
            recv_sem=recv_sem.at[0, step - 1, chunk],
            device_id={"slab": target},
            device_id_type=MESH,
        )

    def back_copy(step, chunk, target, source):
        return pltpu.make_async_remote_copy(
            src_ref=lines_back.at[:, :, chunk, row_block(target), :],
            dst_ref=planes_back.at[:, :, source * own_lines + chunk],
            send_sem=send_sem.at[1, step - 1, chunk],
            recv_sem=recv_sem.at[1, step - 1, chunk],
            device_id={"slab": target},
            device_id_type=MESH,
        )

    def to(step):
        return lax.rem(slab + step, slabs)

    def come_from(step):
        return lax.rem(slab + slabs - step, slabs)

    coupling = (REFERENCE_LAME + REFERENCE_SHEAR) / (
        REFERENCE_SHEAR * (REFERENCE_LAME + 2.0 * REFERENCE_SHEAR)
    )
    middle = GRID // 2

    def signed(index):
        wrapped = jnp.where(index < middle, index, index - GRID)
        return jnp.where(index == middle, 0, wrapped)

    def line_stage(chunk):
        stacked = jnp.concatenate(
            [lines[n, :, chunk].reshape(2 * GRID, LANES) for n in range(6)], axis=1
        )
        high, low = halves(stacked)
        work[...] = mul(line_ref[0], high) + mul(line_ref[0], low) + mul(line_ref[1], high)
        index_y = slab * own_lines + chunk + ROUGH * ((group >> 1) + 2 * (group & 1))
        index_z = lane & (LANES // GROUPS - 1)
        freq_y = signed(index_y)
        freq_z = index_z

        @pl.loop(0, GRID // 8)
        def _(block):
            index_x = block * 8 + lax.broadcasted_iota(jnp.int32, (8, 1), 0)
            freq_x = signed(index_x)
            length = freq_x * freq_x + (freq_y * freq_y + freq_z * freq_z)
            keep = (index_x != middle) & (index_y != middle) & (length > 0)
            inverse = jnp.where(keep, 1.0 / jnp.maximum(length, 1).astype(jnp.float32), 0.0)
            scale = inverse * (1.0 / REFERENCE_SHEAR)
            along = coupling * inverse * inverse
            xi = [freq.astype(jnp.float32) for freq in (freq_x, freq_y, freq_z)]
            for part in range(2):
                picked = pl.ds(pl.multiple_of(part * GRID + block * 8, 8), 8)
                tau = [work[picked, n * LANES : (n + 1) * LANES] for n in range(6)]
                load = [
                    tau[row[0]] * xi[0] + tau[row[1]] * xi[1] + tau[row[2]] * xi[2]
                    for row in TENSOR_ROWS
                ]
                normal = (xi[0] * load[0] + xi[1] * load[1] + xi[2] * load[2]) * along
                field = [0.5 * (load[d] * scale - xi[d] * normal) for d in range(3)]
                for n, (left, right) in enumerate(TENSOR_PAIRS):
                    value = xi[left] * field[right] + xi[right] * field[left]
                    work[picked, n * LANES : (n + 1) * LANES] = value

        high, low = halves(work[...])
        result = (
            mul(line_back_ref[0], high) + mul(line_back_ref[0], low) + mul(line_back_ref[1], high)
        )
        for n in range(6):
            lines_back[n, :, chunk] = result[:, n * LANES : (n + 1) * LANES].reshape(
                2, GRID, LANES
            )

    @pl.loop(0, ITERS)
    def _(iteration):
        @pl.loop(0, ROUGH)
        def _(block):
            at = lane_block(block)
            stress = voxel_law(
                [elastic[n, :, at] for n in range(6)],
                phase_ref[:, at],
                flag_ref[iteration, :, at],
                False,
            )
            high, low = halves(jnp.concatenate(stress, axis=0))
            result = mul(high, depth_ref[0]) + mul(low, depth_ref[0]) + mul(high, depth_ref[1])
            for n in range(6):
                piece = result[n * rows : (n + 1) * rows]
                planes[n, 0, block] = piece[:, :LANES]
                planes[n, 1, block] = piece[:, LANES:]

        sixteen(planes, -1)

        @pl.when(iteration == 0)
        def _():
            pl.semaphore_wait(barrier, slabs - 1 + points - 1)

        for chunk in range(own_lines):
            for step in list(range(1, slabs)) + [0]:
                target = to(step)
                line = target * own_lines + chunk
                cosine, sine = twiddle_ref[line, 0:1, :], twiddle_ref[line, 1:2, :]
                for n in range(6):
                    re, im = groups_forward(
                        planes[n, 0, line], planes[n, 1, line], cosine, sine
                    )
                    if step:
                        planes[n, 0, line] = re
                        planes[n, 1, line] = im
                    else:
                        lines[n, 0, chunk, row_block(slab), :] = re
                        lines[n, 1, chunk, row_block(slab), :] = im
                if step:
                    forward_copy(step, chunk, target, slab).start()

        @pl.loop(0, own_lines)
        def _(chunk):
            for step in range(1, slabs):
                forward_copy(step, chunk, to(step), come_from(step)).wait_recv()
            line_stage(chunk)
            for step in range(1, slabs):
                back_copy(step, chunk, to(step), slab).start()

        @pl.loop(0, own_lines)
        def _(chunk):
            for step in range(slabs):
                source = come_from(step)
                line = source * own_lines + chunk
                if step:
                    back_copy(step, chunk, to(step), source).wait_recv()
                cosine, sine = twiddle_ref[line, 0:1, :], twiddle_ref[line, 1:2, :]
                for n in range(6):
                    if step:
                        re, im = planes_back[n, 0, line], planes_back[n, 1, line]
                    else:
                        re = lines_back[n, 0, chunk, row_block(slab), :]
                        im = lines_back[n, 1, chunk, row_block(slab), :]
                    re, im = groups_back(re, im, cosine, sine)
                    planes_back[n, 0, line] = re
                    planes_back[n, 1, line] = im

        @pl.loop(0, own_lines)
        def _(chunk):
            for step in range(1, slabs):
                forward_copy(step, chunk, to(step), slab).wait_send()
                back_copy(step, chunk, to(step), slab).wait_send()

        sixteen(planes_back, 1)

        @pl.loop(0, ROUGH)
        def _(block):
            at = lane_block(block)
            stacked = jnp.concatenate(
                [
                    jnp.concatenate([planes_back[n, 0, block], planes_back[n, 1, block]], axis=1)
                    for n in range(6)
                ],
                axis=0,
            )
            high, low = halves(stacked)
            result = (
                mul(high, depth_back_ref[0])
                + mul(low, depth_back_ref[0])
                + mul(high, depth_back_ref[1])
            )
            for n in range(6):
                elastic[n, :, at] = elastic[n, :, at] - result[n * rows : (n + 1) * rows]

    sums[...] = jnp.zeros_like(sums)

    @pl.loop(0, ROUGH)
    def _(block):
        at = lane_block(block)
        stress, trial, shear, beta = voxel_law(
            [elastic[n, :, at] for n in range(6)], phase_ref[:, at], flag_ref[ITERS, :, at], True
        )
        entries = stress + [shear]
        for a in range(6):
            weighted = beta * trial[a]
            for b in range(a, 6):
                entries.append(weighted * trial[b])
        for place, value in enumerate(entries):
            folded = value[:, :LANES] + value[:, LANES:]
            total = folded[0:8]
            for half in range(1, rows // 8):
                total = total + folded[half * 8 : half * 8 + 8]
            sums[place] = sums[place] + total

    slab_sums[slab] = jnp.sum(sums[...], axis=1)

    def slab_copy(step, source):
        return pltpu.make_async_remote_copy(
            src_ref=slab_sums.at[source],
            dst_ref=slab_sums.at[source],
            send_sem=slab_send.at[step - 1],
            recv_sem=slab_recv.at[step - 1],
            device_id={"slab": to(step)},
            device_id_type=MESH,
        )

    def point_copy(step, source):
        return pltpu.make_async_remote_copy(
            src_ref=point_sums.at[source],
            dst_ref=point_sums.at[source],
            send_sem=point_send.at[step - 1],
            recv_sem=point_recv.at[step - 1],
            device_id={"rve": lax.rem(point + step, points)},
            device_id_type=MESH,
        )

    for step in range(1, slabs):
        slab_copy(step, slab).start()
    for step in range(1, slabs):
        slab_copy(step, come_from(step)).wait_recv()
    total = slab_sums[0]
    for other in range(1, slabs):
        total = total + slab_sums[other]
    point_sums[point] = jnp.broadcast_to(
        jnp.sum(total, axis=1, keepdims=True), (STATS, LANES)
    )
    for step in range(1, points):
        point_copy(step, point).start()
    for step in range(1, points):
        point_copy(step, lax.rem(point + points - step, points)).wait_recv()
    out_ref[...] = point_sums[...]
    for step in range(1, slabs):
        slab_copy(step, slab).wait_send()
    for step in range(1, points):
        point_copy(step, point).wait_send()


def fused_on_device(phase_ids, yield_flags, plastic_strain, displacements, connectivity):
    slabs = lax.axis_size("slab")
    points = lax.axis_size("rve")
    rows = phase_ids.shape[0]
    node_count = displacements.shape[0]
    element_count = connectivity.shape[0]
    own_lines = ROUGH // slabs
    point = lax.axis_index("rve")
    lookup = gradient_table()
    placing = (
        connectivity[:, :, None] == jnp.arange(node_count, dtype=jnp.int32)[None, None, :]
    ).astype(jnp.float32)
    corner_moves = jnp.sum(placing[:, :, :, None] * displacements[None, None, :, :], axis=2)
    all_strain = jnp.sum(
        jnp.asarray(lookup, jnp.float32)[None] * corner_moves.reshape(element_count, 1, 1, 24),
        axis=3,
    ).reshape(points, 6)
    macro_strain = lax.dynamic_slice(all_strain, (point, 0), (1, 6))[0]

    depth, depth_back = depth_tables()
    line, line_back = line_tables()
    wide = GROUPS * GRID
    vmem = pl.BlockSpec(memory_space=pltpu.VMEM)
    stats = pl.pallas_call(
        lambda *refs: cell_kernel(slabs, points, *refs),
        out_shape=jax.ShapeDtypeStruct((points, STATS, LANES), jnp.float32),
        in_specs=[pl.BlockSpec(memory_space=pltpu.SMEM)] + [vmem] * 8,
        out_specs=vmem,
        scratch_shapes=[
            pltpu.VMEM((6, rows, GRID * GRID), jnp.float32),
            pltpu.VMEM((6, 2, ROUGH, rows, LANES), jnp.float32),
            pltpu.VMEM((6, 2, own_lines, GRID, LANES), jnp.float32),
            pltpu.VMEM((6, 2, own_lines, GRID, LANES), jnp.float32),
            pltpu.VMEM((6, 2, ROUGH, rows, LANES), jnp.float32),
            pltpu.VMEM((2 * GRID, 6 * LANES), jnp.float32),
            pltpu.VMEM((STATS, 8, LANES), jnp.float32),
            pltpu.VMEM((slabs, STATS, LANES), jnp.float32),
            pltpu.VMEM((points, STATS, LANES), jnp.float32),
            pltpu.SemaphoreType.DMA((2, slabs - 1, own_lines)),
            pltpu.SemaphoreType.DMA((2, slabs - 1, own_lines)),
            pltpu.SemaphoreType.DMA((slabs - 1,)),
            pltpu.SemaphoreType.DMA((slabs - 1,)),
            pltpu.SemaphoreType.DMA((points - 1,)),
            pltpu.SemaphoreType.DMA((points - 1,)),
        ],
        compiler_params=pltpu.CompilerParams(
            collective_id=0, has_side_effects=True, vmem_limit_bytes=40 * 1024 * 1024
        ),
    )(
        macro_strain,
        phase_ids,
        yield_flags[0],
        plastic_strain[0],
        host_halves(depth),
        host_halves(depth_back),
        host_halves(line),
        host_halves(line_back),
        twiddle_table(),
    )
    means = stats[:, :, 0] / float(GRID**3)
    mean_stress = means[:, :6]
    pair_place = np.zeros((6, 6), np.int32)
    place = 7
    for a in range(6):
        for b in range(a, 6):
            pair_place[a, b] = pair_place[b, a] = place
            place += 1
    outer = jnp.stack([means[:, place] for place in pair_place.reshape(-1)], axis=1)
    outer = outer.reshape(points, 6, 6)
    tangent = jax.vmap(tangent_matrix)(means[:, 6], outer)
    weights = np.asarray(PAIR_WEIGHTS)
    weighted = lookup * weights[None, :, None] * QUADRATURE_WEIGHT
    weighted = jnp.asarray(weighted.reshape(48, 24), jnp.float32)
    element_force = jnp.sum(
        mean_stress.reshape(element_count, 48, 1) * weighted[None], axis=1
    )
    best = lax.Precision.HIGHEST
    spread = jnp.einsum(
        "equn,qnv->equv",
        tangent.reshape(element_count, 8, 6, 6),
        jnp.asarray(lookup, jnp.float32),
        precision=best,
    ).reshape(element_count, 48, 24)
    element_stiffness = jnp.einsum("rh,erv->ehv", weighted, spread, precision=best)
    forces = jnp.einsum(
        "eck,ecn->nk", element_force.reshape(element_count, 8, 3), placing, precision=best
    )
    block = element_stiffness.reshape(element_count, 8, 3, 8, 3)
    stiffness = jnp.einsum("ecn,eckdl,edm->nkml", placing, block, placing, precision=best)
    stiffness = stiffness.reshape(3 * node_count, 3 * node_count)
    own_stress = lax.dynamic_slice(mean_stress, (point, 0), (1, 6))
    own_tangent = lax.dynamic_slice(tangent, (point, 0, 0), (1, 6, 6))
    return (own_stress, own_tangent, forces, stiffness)


def solution(mesh):
    slabs = mesh.shape["slab"]
    fits = slabs > 1 and ROUGH % slabs == 0 and GRID // slabs % 8 == 0
    body = fused_on_device if fits else on_device
    return jax.shard_map(
        body,
        mesh=mesh,
        in_specs=(
            P("slab", None),
            P("rve", None, "slab", None),
            P("rve", None, "slab", None),
            P(),
            P(),
        ),
        out_specs=(P("rve", None), P("rve", None, None), P(), P()),
        check_vma=False,
    )
```

```python
import math

import jax
import jax.numpy as jnp
import numpy as np
from jax import lax
from jax.experimental import pallas as pl
from jax.experimental.pallas import tpu as pltpu
from jax.sharding import PartitionSpec as P

GRID = 64
ITERS = 2


SHEAR_MODULUS = 80.0
BULK_MODULUS = 160.0
REFERENCE_SHEAR = 80.0
REFERENCE_LAME = 160.0 - 160.0 / 3.0
TANGENT_UNIT = 100.0
QUADRATURE_WEIGHT = 0.125
DIAGONAL_PART = (1.0, 1.0, 1.0, 0.0, 0.0, 0.0)
PAIR_WEIGHTS = (1.0, 1.0, 1.0, 2.0, 2.0, 2.0)
TENSOR_PAIRS = ((0, 0), (1, 1), (2, 2), (1, 2), (0, 2), (0, 1))
TENSOR_ROWS = ((0, 5, 4), (5, 1, 3), (4, 3, 2))


def gradient_table():
    inverse_root = 1.0 / math.sqrt(3.0)
    table_rows = np.zeros((8, 6, 24))
    for gauss_corner in range(8):
        position = [
            0.5 + (2 * (gauss_corner >> axis_number & 1) - 1) * 0.5 * inverse_root
            for axis_number in range(3)
        ]
        for corner in range(8):
            corner_bits = [corner >> axis_number & 1 for axis_number in range(3)]
            factors = [
                position[axis_number] * corner_bits[axis_number]
                + (1.0 - position[axis_number]) * (1 - corner_bits[axis_number])
                for axis_number in range(3)
            ]
            slopes = []
            for axis_number in range(3):
                slope_value = 2.0 * corner_bits[axis_number] - 1.0
                for other_axis in range(3):
                    if other_axis != axis_number:
                        slope_value = slope_value * factors[other_axis]
                slopes.append(slope_value)
            column = 3 * corner
            table_rows[gauss_corner, 0, column] += slopes[0]
            table_rows[gauss_corner, 1, column + 1] += slopes[1]
            table_rows[gauss_corner, 2, column + 2] += slopes[2]
            table_rows[gauss_corner, 3, column + 1] += 0.5 * slopes[2]
            table_rows[gauss_corner, 3, column + 2] += 0.5 * slopes[1]
            table_rows[gauss_corner, 4, column] += 0.5 * slopes[2]
            table_rows[gauss_corner, 4, column + 2] += 0.5 * slopes[0]
            table_rows[gauss_corner, 5, column] += 0.5 * slopes[1]
            table_rows[gauss_corner, 5, column + 1] += 0.5 * slopes[0]
    return table_rows


def point_geometry(points, connectivity, corner_lookup, node_count):
    element_count = connectivity.shape[0]
    point_count = points.shape[0]
    corner_selector = (points[:, None] % 8 == jnp.arange(8, dtype=jnp.int32)[None, :]).astype(
        jnp.float32
    )
    strain_row_values = jnp.einsum(
        "zu,utf->ztf", corner_selector, corner_lookup, precision=lax.Precision.HIGHEST
    )
    element_onehot = points[:, None] // 8 == jnp.arange(element_count, dtype=jnp.int32)[None, :]
    corner_nodes = jnp.sum(
        jnp.where(element_onehot[:, :, None], connectivity[None, :, :], 0), axis=1
    )
    degrees = 3 * corner_nodes[:, :, None] + jnp.arange(3, dtype=jnp.int32)[None, None, :]
    degrees = degrees.reshape(point_count, 24)
    placing = (
        degrees[:, :, None] == jnp.arange(3 * node_count, dtype=jnp.int32)[None, None, :]
    ).astype(jnp.float32)
    return (strain_row_values, placing)


def macro_strains(strain_row_values, placing, displacements):
    nodal_quantities = jnp.einsum(
        "gpn,n->gp", placing, displacements.reshape(-1), precision=lax.Precision.HIGHEST
    )
    return jnp.einsum(
        "vxw,vw->vx", strain_row_values, nodal_quantities, precision=lax.Precision.HIGHEST
    )


def material_response(strain, plastic, phase_ids, flag_values):
    diagonal = jnp.asarray(DIAGONAL_PART, jnp.float32)[:, None]
    weights = jnp.asarray(PAIR_WEIGHTS, jnp.float32)[:, None]
    martensite = phase_ids == 1
    yield_stress = jnp.where(martensite, 1.2, 0.3).astype(jnp.float32)
    hardening = jnp.where(martensite, 10.0, 2.0).astype(jnp.float32)
    elastic = strain - plastic
    volume = elastic[0] + elastic[1] + elastic[2]
    trial_dev = 2.0 * SHEAR_MODULUS * (elastic - diagonal * (volume / 3.0))
    equivalent = jnp.sqrt(1.5 * jnp.sum(weights * trial_dev * trial_dev, axis=0))
    bounded = jnp.maximum(equivalent, yield_stress)
    return_ratio = 3.0 * SHEAR_MODULUS / (3.0 * SHEAR_MODULUS + hardening)
    active = flag_values.astype(jnp.float32)
    plastic_flow = active * (equivalent - yield_stress) / bounded
    softening = 1.0 - return_ratio * plastic_flow
    stress = trial_dev * softening + diagonal * (BULK_MODULUS * volume)
    shear_term = 2.0 * SHEAR_MODULUS * softening
    tangent_weight = (
        3.0 * SHEAR_MODULUS * return_ratio * active * yield_stress / (bounded * bounded * bounded)
    )
    return (stress, trial_dev, shear_term, tangent_weight)


def wave_terms(index_x, index_y, index_z):
    middle = GRID // 2
    signed = []
    for indices in (index_x, index_y, index_z):
        wrapped = jnp.where(indices < middle, indices, indices - GRID)
        signed.append(jnp.where(indices == middle, 0, wrapped))
    nyquist_free = (index_x != middle) & (index_y != middle) & (index_z != middle)
    length = signed[0] * signed[0] + signed[1] * signed[1] + signed[2] * signed[2]
    keep_mask = (nyquist_free & (length > 0)).astype(jnp.float32)
    inverse_length = 1.0 / jnp.sqrt(jnp.maximum(length, 1).astype(jnp.float32))
    normals = [signed_entry.astype(jnp.float32) * inverse_length for signed_entry in signed]
    return (normals, keep_mask)


def project_green(components, normals, keep_mask):
    traction = [
        components[tensor_row[0]] * normals[0]
        + components[tensor_row[1]] * normals[1]
        + components[tensor_row[2]] * normals[2]
        for tensor_row in TENSOR_ROWS
    ]
    normal_load = normals[0] * traction[0] + normals[1] * traction[1] + normals[2] * traction[2]
    coupling = (REFERENCE_LAME + REFERENCE_SHEAR) / (
        REFERENCE_SHEAR * (REFERENCE_LAME + 2.0 * REFERENCE_SHEAR)
    )
    result_list = []
    for left_axis, right_axis in TENSOR_PAIRS:
        entry_value = (
            normals[left_axis] * traction[right_axis] + normals[right_axis] * traction[left_axis]
        ) / (2.0 * REFERENCE_SHEAR)
        entry_value = (
            entry_value - coupling * normals[left_axis] * normals[right_axis] * normal_load
        )
        result_list.append(entry_value * keep_mask)
    return jnp.stack(result_list)


def tangent_matrix(mean_shear, outer_sum):
    diagonal = jnp.asarray(DIAGONAL_PART, jnp.float32)
    volumetric = diagonal[:, None] * diagonal[None, :]
    weights = jnp.asarray(PAIR_WEIGHTS, jnp.float32)
    identity = jnp.eye(6, dtype=jnp.float32)
    whole = (
        BULK_MODULUS * volumetric
        + mean_shear * (identity - volumetric / 3.0)
        - outer_sum * weights[None, :]
    )
    return whole / TANGENT_UNIT


def assemble(stress_values, tangent_moduli, strain_row_values, placing):
    weights = jnp.asarray(PAIR_WEIGHTS, jnp.float32)
    force_row_values = strain_row_values * weights[None, :, None]
    element_force_vector = QUADRATURE_WEIGHT * jnp.einsum(
        "mbh,mb->mh", force_row_values, stress_values, precision=lax.Precision.HIGHEST
    )
    element_stiffness_matrix = QUADRATURE_WEIGHT * jnp.einsum(
        "xoh,xon,xnv->xhv",
        force_row_values,
        tangent_moduli,
        strain_row_values,
        precision=lax.Precision.HIGHEST,
    )
    forces = jnp.einsum("gp,gpn->n", element_force_vector, placing, precision=lax.Precision.HIGHEST)
    stiffness = jnp.einsum(
        "gpq,gpm,gqn->mn",
        element_stiffness_matrix,
        placing,
        placing,
        precision=lax.Precision.HIGHEST,
    )
    return (forces.reshape(-1, 3), stiffness)


def angle_table(count_rows, count_cols):
    rows_index = lax.broadcasted_iota(jnp.int32, (count_rows, count_cols), 0)
    cols_index = lax.broadcasted_iota(jnp.int32, (count_rows, count_cols), 1)
    angles = 2.0 * math.pi / GRID * (rows_index * cols_index % GRID).astype(jnp.float32)
    return (jnp.cos(angles), jnp.sin(angles))


def complex_table(inverse):
    cosine, sine = angle_table(GRID, GRID)
    if inverse:
        first_row = jnp.stack([cosine, -sine], axis=1)
        second_row = jnp.stack([sine, cosine], axis=1)
    else:
        first_row = jnp.stack([cosine, sine], axis=1)
        second_row = jnp.stack([-sine, cosine], axis=1)
    return jnp.stack([first_row, second_row], axis=0)


def on_device(phase_ids, yield_flags, plastic_strain, displacements, connectivity):
    slabs = lax.axis_size("slab")
    slab_index = lax.axis_index("slab")
    plane_count = phase_ids.shape[0]
    row_planes = GRID // slabs
    node_count = displacements.shape[0]
    corner_lookup = jnp.asarray(gradient_table(), jnp.float32)
    gauss_point = lax.axis_index("rve")
    own_points = jnp.full((1,), gauss_point, jnp.int32)
    strain_row_values, placing = point_geometry(own_points, connectivity, corner_lookup, node_count)
    macro_strain = macro_strains(strain_row_values, placing, displacements)[0]
    phases = phase_ids.reshape(-1)
    plastic = plastic_strain[0].reshape(6, -1)
    point_flags = yield_flags[0]
    columns = GRID // 2
    kept_index = lax.broadcasted_iota(jnp.int32, (columns, 1), 0)
    column_weight = jnp.where(kept_index == 0, 1.0, 2.0).astype(jnp.float32)
    depth_cos, depth_sin = angle_table(columns, GRID)
    forward_depth = jnp.stack([depth_cos, -depth_sin], axis=0)
    inverse_depth = jnp.stack(
        [column_weight * depth_cos, -column_weight * depth_sin], axis=0
    ) / float(GRID**3)
    forward_plane = complex_table(False)
    inverse_plane = complex_table(True)
    index_x = lax.broadcasted_iota(jnp.int32, (GRID, 1, 1), 0)
    index_y = slab_index * row_planes + lax.broadcasted_iota(jnp.int32, (1, row_planes, 1), 1)
    index_z = lax.broadcasted_iota(jnp.int32, (1, 1, columns), 2)
    normals, keep_mask = wave_terms(index_x, index_y, index_z)
    strain = jnp.broadcast_to(macro_strain[:, None], plastic.shape)
    for iteration in range(ITERS):
        stress = material_response(strain, plastic, phases, point_flags[iteration].reshape(-1))[0]
        voxel_block = stress.reshape(6, plane_count, GRID, GRID)
        spectral = jnp.einsum(
            "pkz,cxyz->pcxyk", forward_depth, voxel_block, precision=lax.Precision.HIGHEST
        )
        spectral = jnp.einsum(
            "pjqy,qcxyk->pcxjk", forward_plane, spectral, precision=lax.Precision.HIGHEST
        )
        spectral = lax.all_to_all(spectral, "slab", split_axis=3, concat_axis=2, tiled=True)
        spectral = jnp.einsum(
            "pjqx,qcxyk->pcjyk", forward_plane, spectral, precision=lax.Precision.HIGHEST
        )
        projected = project_green(
            [spectral[:, component] for component in range(6)], normals, keep_mask
        )
        spectral = jnp.einsum(
            "pjqx,cqxyk->pcjyk", inverse_plane, projected, precision=lax.Precision.HIGHEST
        )
        spectral = lax.all_to_all(spectral, "slab", split_axis=2, concat_axis=3, tiled=True)
        spectral = jnp.einsum(
            "pjqy,qcxyk->pcxjk", inverse_plane, spectral, precision=lax.Precision.HIGHEST
        )
        correction = jnp.einsum(
            "pkz,pcxyk->cxyz", inverse_depth, spectral, precision=lax.Precision.HIGHEST
        )
        strain = strain - correction.reshape(6, -1)
    stress, trial_dev, shear_term, tangent_weight = material_response(
        strain, plastic, phases, point_flags[ITERS].reshape(-1)
    )
    outer_part = jnp.dot(
        trial_dev * tangent_weight[None, :], trial_dev.T, precision=lax.Precision.HIGHEST
    )
    stress_total, shear_total, outer_total = lax.psum(
        (jnp.sum(stress, axis=1), jnp.sum(shear_term), outer_part), "slab"
    )
    voxel_count = float(GRID**3)
    mean_stress = stress_total / voxel_count
    tangent = tangent_matrix(shear_total / voxel_count, outer_total / voxel_count)
    own_forces, own_stiffness = assemble(
        mean_stress[None], tangent[None], strain_row_values, placing
    )
    forces, stiffness = lax.psum((own_forces, own_stiffness), "rve")
    return (mean_stress[None], tangent[None], forces, stiffness)


ROUGH = 16
GROUPS = 4
LANES = 128
STATS = 32
MESH = pl.DeviceIdType.MESH


def halves(value):
    high = value.astype(jnp.bfloat16)
    return high, (value - high.astype(jnp.float32)).astype(jnp.bfloat16)


def mul(left, right):
    return jnp.dot(left, right, preferred_element_type=jnp.float32)


def host_halves(table):
    table = np.asarray(table, np.float32)
    high = table.astype(jnp.bfloat16)
    low = (table - high.astype(np.float32)).astype(jnp.bfloat16)
    return np.stack([high, low])


def depth_tables():
    kept = GRID // 2
    angles = 2.0 * np.pi / GRID * (np.arange(GRID)[:, None] * np.arange(kept)[None, :] % GRID)
    weight = np.where(np.arange(kept) == 0, 1.0, 2.0) / float(GRID**3)
    eye = np.eye(GROUPS)
    forward = np.concatenate([np.kron(eye, np.cos(angles)), np.kron(eye, -np.sin(angles))], axis=1)
    back_cos = (np.cos(angles) * weight[None, :]).T
    back_sin = (-np.sin(angles) * weight[None, :]).T
    inverse = np.concatenate([np.kron(eye, back_cos), np.kron(eye, back_sin)], axis=0)
    return forward, inverse


def line_tables():
    angles = 2.0 * np.pi / GRID * (np.arange(GRID)[:, None] * np.arange(GRID)[None, :] % GRID)
    cosine, sine = np.cos(angles), np.sin(angles)
    forward = np.block([[cosine, sine], [-sine, cosine]])
    inverse = np.block([[cosine, -sine], [sine, cosine]])
    return forward, inverse


def twiddle_table():
    lane_group = np.arange(LANES) // (LANES // GROUPS)
    angles = 2.0 * np.pi / GRID * (np.arange(ROUGH)[:, None] * lane_group[None, :])
    return jnp.asarray(np.stack([np.cos(angles), -np.sin(angles)], axis=1), jnp.float32)


def four_point(re, im, sign):
    a_re, a_im = re[0] + re[2], im[0] + im[2]
    b_re, b_im = re[0] - re[2], im[0] - im[2]
    c_re, c_im = re[1] + re[3], im[1] + im[3]
    d_re, d_im = re[1] - re[3], im[1] - im[3]
    e_re, e_im = (d_im, -d_re) if sign < 0 else (-d_im, d_re)
    return (
        [a_re + c_re, b_re + e_re, a_re - c_re, b_re - e_re],
        [a_im + c_im, b_im + e_im, a_im - c_im, b_im - e_im],
    )


def sixteen_point(re, im, sign):
    inner_re, inner_im = [], []
    for b in range(4):
        part_re, part_im = four_point(re[b::4], im[b::4], sign)
        for ka in range(1, 4):
            if b:
                angle = 2.0 * math.pi * b * ka / 16.0
                cosine, sine = math.cos(angle), sign * math.sin(angle)
                old_re, old_im = part_re[ka], part_im[ka]
                part_re[ka] = old_re * cosine - old_im * sine
                part_im[ka] = old_re * sine + old_im * cosine
        inner_re.append(part_re)
        inner_im.append(part_im)
    out_re, out_im = [None] * 16, [None] * 16
    for ka in range(4):
        part_re, part_im = four_point(
            [inner_re[b][ka] for b in range(4)], [inner_im[b][ka] for b in range(4)], sign
        )
        for kb in range(4):
            out_re[ka + 4 * kb] = part_re[kb]
            out_im[ka + 4 * kb] = part_im[kb]
    return out_re, out_im


def voxel_law(elastic, phase, flag, want_tangent):
    martensite = phase == 1
    yield_stress = jnp.where(martensite, 1.2, 0.3).astype(jnp.float32)
    base = 3.0 * SHEAR_MODULUS
    ratio = jnp.where(martensite, base / (base + 10.0), base / (base + 2.0)).astype(jnp.float32)
    volume = elastic[0] + elastic[1] + elastic[2]
    third = volume * (1.0 / 3.0)
    trial = [
        (2.0 * SHEAR_MODULUS) * (elastic[n] - third if n < 3 else elastic[n]) for n in range(6)
    ]
    square = [value * value for value in trial]
    norm = square[0] + square[1] + square[2] + 2.0 * (square[3] + square[4] + square[5])
    equivalent = jnp.sqrt(1.5 * norm)
    bounded = jnp.maximum(equivalent, yield_stress)
    active = flag.astype(jnp.float32)
    inverse = 1.0 / bounded
    active_ratio = active * ratio
    softening = 1.0 - active_ratio * ((equivalent - yield_stress) * inverse)
    pressure = BULK_MODULUS * volume
    stress = [trial[n] * softening + pressure if n < 3 else trial[n] * softening for n in range(6)]
    if not want_tangent:
        return stress
    beta = base * active_ratio * yield_stress * (inverse * inverse * inverse)
    return stress, trial, (2.0 * SHEAR_MODULUS) * softening, beta


def cell_kernel(
    slabs, points, macro_ref, phase_hbm, flag_hbm, plastic_hbm, depth_hbm, line_hbm, twiddle_hbm,
    out_ref,
    phase_ref, flag_ref, depth_ref, line_ref, twiddle_ref,
    elastic, planes, lines, lines_back, planes_back, work, sums, slab_sums, point_sums,
    load_sem, send_sem, recv_sem, slab_send, slab_recv, point_send, point_recv,
):
    slab = lax.axis_index("slab")
    point = lax.axis_index("rve")
    rows = GRID // slabs
    own_lines = ROUGH // slabs
    wide = GROUPS * GRID

    barrier = pltpu.get_barrier_semaphore()
    for step in range(1, slabs):
        pl.semaphore_signal(
            barrier, inc=1, device_id={"slab": lax.rem(slab + step, slabs)}, device_id_type=MESH
        )
    for step in range(1, points):
        pl.semaphore_signal(
            barrier, inc=1, device_id={"rve": lax.rem(point + step, points)}, device_id_type=MESH
        )

    def lane_block(index):
        return pl.ds(pl.multiple_of(index * wide, wide), wide)

    def row_block(index):
        return pl.ds(pl.multiple_of(index * rows, rows), rows)

    parts = rows // 8

    def part_rows(part):
        return pl.ds(pl.multiple_of(part * 8, 8), 8)

    pairs = [
        (plastic_hbm.at[:, 0:8], elastic.at[:, 0:8]),
        (phase_hbm, phase_ref),
        (flag_hbm.at[0], flag_ref.at[0]),
        (depth_hbm, depth_ref),
        (twiddle_hbm, twiddle_ref),
        (plastic_hbm.at[:, 8:rows], elastic.at[:, 8:rows]),
        (line_hbm, line_ref),
        (flag_hbm.at[1:], flag_ref.at[1:]),
    ]
    loads = [
        pltpu.make_async_copy(source, target, load_sem.at[place])
        for place, (source, target) in enumerate(pairs)
    ]
    for load in loads:
        load.start()

    lane = lax.broadcasted_iota(jnp.int32, (1, LANES), 1)
    group = lane >> 5
    high_sign = jnp.where((group >> 1) == 0, 1.0, -1.0).astype(jnp.float32)
    low_sign = jnp.where((group & 1) == 0, 1.0, -1.0).astype(jnp.float32)
    low_first = (group & 1) == 0
    corner = group == 3

    def across_high(value):
        return pltpu.roll(value, 64, 1) + high_sign * value

    def across_low(value):
        partner = jnp.where(low_first, pltpu.roll(value, 96, 1), pltpu.roll(value, 32, 1))
        return partner + low_sign * value

    def groups_forward(re, im, cosine, sine):
        re, im = re * cosine - im * sine, re * sine + im * cosine
        re, im = across_high(re), across_high(im)
        re, im = jnp.where(corner, im, re), jnp.where(corner, -re, im)
        return across_low(re), across_low(im)

    def groups_back(re, im, cosine, sine):
        re, im = across_low(re), across_low(im)
        re, im = jnp.where(corner, -im, re), jnp.where(corner, re, im)
        re, im = across_high(re), across_high(im)
        return re * cosine + im * sine, im * cosine - re * sine

    def sixteen(ref, sign, part):
        @pl.loop(0, 6)
        def _(n):
            picked = part_rows(part)
            re = [ref[n, 0, k, picked, :] for k in range(ROUGH)]
            im = [ref[n, 1, k, picked, :] for k in range(ROUGH)]
            re, im = sixteen_point(re, im, sign)
            for k in range(ROUGH):
                ref[n, 0, k, picked, :] = re[k]
                ref[n, 1, k, picked, :] = im[k]

    def slab_rows(index, part):
        return pl.ds(pl.multiple_of(index * rows + part * 8, 8), 8)

    def forward_copy(step, chunk, part, target, source):
        return pltpu.make_async_remote_copy(
            src_ref=planes.at[:, :, target * own_lines + chunk, part_rows(part), :],
            dst_ref=lines.at[:, :, chunk, slab_rows(source, part), :],
            send_sem=send_sem.at[0, part, step - 1, chunk],
            recv_sem=recv_sem.at[0, part, step - 1, chunk],
            device_id={"slab": target},
            device_id_type=MESH,
        )

    def back_copy(step, chunk, part, target, source):
        return pltpu.make_async_remote_copy(
            src_ref=lines_back.at[:, :, chunk, slab_rows(target, part), :],
            dst_ref=planes_back.at[:, :, source * own_lines + chunk, part_rows(part), :],
            send_sem=send_sem.at[1, part, step - 1, chunk],
            recv_sem=recv_sem.at[1, part, step - 1, chunk],
            device_id={"slab": target},
            device_id_type=MESH,
        )

    def to(step):
        return lax.rem(slab + step, slabs)

    def come_from(step):
        return lax.rem(slab + slabs - step, slabs)

    coupling = (REFERENCE_LAME + REFERENCE_SHEAR) / (
        REFERENCE_SHEAR * (REFERENCE_LAME + 2.0 * REFERENCE_SHEAR)
    )
    middle = GRID // 2

    def signed(index):
        wrapped = jnp.where(index < middle, index, index - GRID)
        return jnp.where(index == middle, 0, wrapped)

    def line_stage(chunk):
        stacked = jnp.concatenate(
            [lines[n, :, chunk].reshape(2 * GRID, LANES) for n in range(6)], axis=1
        )
        high, low = halves(stacked)
        work[...] = mul(line_ref[0, 0], high) + mul(line_ref[0, 0], low) + mul(line_ref[0, 1], high)
        index_y = slab * own_lines + chunk + ROUGH * ((group >> 1) + 2 * (group & 1))
        index_z = lane & (LANES // GROUPS - 1)
        freq_y = signed(index_y)
        freq_z = index_z

        @pl.loop(0, GRID // 8)
        def _(block):
            index_x = block * 8 + lax.broadcasted_iota(jnp.int32, (8, 1), 0)
            freq_x = signed(index_x)
            length = freq_x * freq_x + (freq_y * freq_y + freq_z * freq_z)
            keep = (index_x != middle) & (index_y != middle) & (length > 0)
            inverse = jnp.where(keep, 1.0 / jnp.maximum(length, 1).astype(jnp.float32), 0.0)
            scale = inverse * (1.0 / REFERENCE_SHEAR)
            along = coupling * inverse * inverse
            xi = [freq.astype(jnp.float32) for freq in (freq_x, freq_y, freq_z)]
            for part in range(2):
                picked = pl.ds(pl.multiple_of(part * GRID + block * 8, 8), 8)
                tau = [work[picked, n * LANES : (n + 1) * LANES] for n in range(6)]
                load = [
                    tau[row[0]] * xi[0] + tau[row[1]] * xi[1] + tau[row[2]] * xi[2]
                    for row in TENSOR_ROWS
                ]
                normal = (xi[0] * load[0] + xi[1] * load[1] + xi[2] * load[2]) * along
                field = [0.5 * (load[d] * scale - xi[d] * normal) for d in range(3)]
                for n, (left, right) in enumerate(TENSOR_PAIRS):
                    value = xi[left] * field[right] + xi[right] * field[left]
                    work[picked, n * LANES : (n + 1) * LANES] = value

        high, low = halves(work[...])
        result = (
            mul(line_ref[1, 0], high) + mul(line_ref[1, 0], low) + mul(line_ref[1, 1], high)
        )
        for n in range(6):
            lines_back[n, :, chunk] = result[:, n * LANES : (n + 1) * LANES].reshape(
                2, GRID, LANES
            )

    def twiddles(line):
        return twiddle_ref[pl.ds(2 * line, 1), :], twiddle_ref[pl.ds(2 * line + 1, 1), :]

    def plane_forward(iteration, part):
        picked = part_rows(part)

        @pl.loop(0, ROUGH // 4)
        def _(batch):
            pieces = []
            for inner in range(4):
                at = lane_block(batch * 4 + inner)
                pieces += voxel_law(
                    [elastic[n, picked, at] for n in range(6)],
                    phase_ref[picked, at],
                    flag_ref[iteration, picked, at],
                    False,
                )
            high, low = halves(jnp.concatenate(pieces, axis=0))
            result = (
                mul(high, depth_ref[0, 0]) + mul(low, depth_ref[0, 0]) + mul(high, depth_ref[0, 1])
            )
            for inner in range(4):
                for n in range(6):
                    first = (inner * 6 + n) * 8
                    planes[n, 0, batch * 4 + inner, picked, :] = result[first : first + 8, :LANES]
                    planes[n, 1, batch * 4 + inner, picked, :] = result[first : first + 8, LANES:]

        sixteen(planes, -1, part)

        @pl.loop(0, own_lines)
        def _(chunk):
            for step in list(range(1, slabs)) + [0]:
                target = to(step)
                line = target * own_lines + chunk
                cosine, sine = twiddles(line)
                for n in range(6):
                    re, im = groups_forward(
                        planes[n, 0, line, picked, :], planes[n, 1, line, picked, :], cosine, sine
                    )
                    if step:
                        planes[n, 0, line, picked, :] = re
                        planes[n, 1, line, picked, :] = im
                    else:
                        lines[n, 0, chunk, slab_rows(slab, part), :] = re
                        lines[n, 1, chunk, slab_rows(slab, part), :] = im
                if step:
                    forward_copy(step, chunk, part, target, slab).start()

    def plane_back(part):
        picked = part_rows(part)

        @pl.loop(0, own_lines)
        def _(chunk):
            for step in range(slabs):
                source = come_from(step)
                line = source * own_lines + chunk
                if step:
                    back_copy(step, chunk, part, to(step), source).wait_recv()
                cosine, sine = twiddles(line)
                for n in range(6):
                    if step:
                        re = planes_back[n, 0, line, picked, :]
                        im = planes_back[n, 1, line, picked, :]
                    else:
                        re = lines_back[n, 0, chunk, slab_rows(slab, part), :]
                        im = lines_back[n, 1, chunk, slab_rows(slab, part), :]
                    re, im = groups_back(re, im, cosine, sine)
                    planes_back[n, 0, line, picked, :] = re
                    planes_back[n, 1, line, picked, :] = im

        sixteen(planes_back, 1, part)

        @pl.loop(0, ROUGH // 4)
        def _(batch):
            stacked = jnp.concatenate(
                [
                    jnp.concatenate(
                        [
                            planes_back[n, side, batch * 4 + inner, picked, :]
                            for inner in range(4)
                            for n in range(6)
                        ],
                        axis=0,
                    )
                    for side in range(2)
                ],
                axis=1,
            )
            high, low = halves(stacked)
            result = (
                mul(high, depth_ref[1, 0]) + mul(low, depth_ref[1, 0]) + mul(high, depth_ref[1, 1])
            )
            for inner in range(4):
                at = lane_block(batch * 4 + inner)
                for n in range(6):
                    first = (inner * 6 + n) * 8
                    elastic[n, picked, at] = elastic[n, picked, at] - result[first : first + 8]

    def final_sums(part):
        picked = part_rows(part)

        @pl.loop(0, ROUGH)
        def _(block):
            at = lane_block(block)
            stress, trial, shear, beta = voxel_law(
                [elastic[n, picked, at] for n in range(6)],
                phase_ref[picked, at],
                flag_ref[ITERS, picked, at],
                True,
            )
            entries = stress + [shear]
            for a in range(6):
                weighted = beta * trial[a]
                for b in range(a, 6):
                    entries.append(weighted * trial[b])
            for place, value in enumerate(entries):
                sums[place] = sums[place] + (value[:, :LANES] + value[:, LANES:])

    sums[...] = jnp.zeros_like(sums)
    for load in loads[:5]:
        load.wait()

    @pl.loop(0, parts)
    def _(part):
        @pl.when(part == 1)
        def _():
            loads[5].wait()

        picked = part_rows(part)

        @pl.loop(0, ROUGH)
        def _(block):
            at = lane_block(block)
            for n in range(6):
                elastic[n, picked, at] = macro_ref[n] - elastic[n, picked, at]

        @pl.when(part == 0)
        def _():
            pl.semaphore_wait(barrier, slabs - 1 + points - 1)

        plane_forward(0, part)

    for load in loads[6:]:
        load.wait()

    @pl.loop(0, ITERS)
    def _(iteration):
        @pl.loop(0, own_lines)
        def _(chunk):
            for step in range(1, slabs):
                for part in range(parts):
                    forward_copy(step, chunk, part, to(step), come_from(step)).wait_recv()
            line_stage(chunk)
            for step in range(1, slabs):
                back_copy(step, chunk, 0, to(step), slab).start()

        @pl.loop(0, own_lines)
        def _(chunk):
            for part in range(1, parts):
                for step in range(1, slabs):
                    back_copy(step, chunk, part, to(step), slab).start()

        @pl.loop(0, parts)
        def _(part):
            plane_back(part)

            @pl.loop(0, own_lines)
            def _(chunk):
                for step in range(1, slabs):
                    forward_copy(step, chunk, part, to(step), slab).wait_send()
                    back_copy(step, chunk, part, to(step), slab).wait_send()

            @pl.when(iteration < ITERS - 1)
            def _():
                plane_forward(iteration + 1, part)

            @pl.when(iteration == ITERS - 1)
            def _():
                final_sums(part)

    slab_sums[slab] = jnp.sum(sums[...], axis=1)

    def slab_copy(step, source):
        return pltpu.make_async_remote_copy(
            src_ref=slab_sums.at[source],
            dst_ref=slab_sums.at[source],
            send_sem=slab_send.at[step - 1],
            recv_sem=slab_recv.at[step - 1],
            device_id={"slab": to(step)},
            device_id_type=MESH,
        )

    def point_copy(step, source):
        return pltpu.make_async_remote_copy(
            src_ref=point_sums.at[source],
            dst_ref=point_sums.at[source],
            send_sem=point_send.at[step - 1],
            recv_sem=point_recv.at[step - 1],
            device_id={"rve": lax.rem(point + step, points)},
            device_id_type=MESH,
        )

    for step in range(1, slabs):
        slab_copy(step, slab).start()
    for step in range(1, slabs):
        slab_copy(step, come_from(step)).wait_recv()
    total = slab_sums[0]
    for other in range(1, slabs):
        total = total + slab_sums[other]
    point_sums[point] = jnp.broadcast_to(
        jnp.sum(total, axis=1, keepdims=True), (STATS, LANES)
    )
    for step in range(1, points):
        point_copy(step, point).start()
    for step in range(1, points):
        point_copy(step, lax.rem(point + points - step, points)).wait_recv()
    out_ref[...] = point_sums[...]
    for step in range(1, slabs):
        slab_copy(step, slab).wait_send()
    for step in range(1, points):
        point_copy(step, point).wait_send()


def fused_on_device(phase_ids, yield_flags, plastic_strain, displacements, connectivity):
    slabs = lax.axis_size("slab")
    points = lax.axis_size("rve")
    rows = phase_ids.shape[0]
    node_count = displacements.shape[0]
    element_count = connectivity.shape[0]
    own_lines = ROUGH // slabs
    point = lax.axis_index("rve")
    lookup = gradient_table()
    placing = (
        connectivity[:, :, None] == jnp.arange(node_count, dtype=jnp.int32)[None, None, :]
    ).astype(jnp.float32)
    corner_moves = jnp.sum(placing[:, :, :, None] * displacements[None, None, :, :], axis=2)
    all_strain = jnp.sum(
        jnp.asarray(lookup, jnp.float32)[None] * corner_moves.reshape(element_count, 1, 1, 24),
        axis=3,
    ).reshape(points, 6)
    macro_strain = lax.dynamic_slice(all_strain, (point, 0), (1, 6))[0]

    depth, depth_back = depth_tables()
    line, line_back = line_tables()
    wide = GROUPS * GRID
    vmem = pl.BlockSpec(memory_space=pltpu.VMEM)
    stats = pl.pallas_call(
        lambda *refs: cell_kernel(slabs, points, *refs),
        out_shape=jax.ShapeDtypeStruct((points, STATS, LANES), jnp.float32),
        in_specs=[pl.BlockSpec(memory_space=pltpu.SMEM)]
        + [pl.BlockSpec(memory_space=pltpu.HBM)] * 6,
        out_specs=vmem,
        scratch_shapes=[
            pltpu.VMEM((rows, GRID * GRID), jnp.int32),
            pltpu.VMEM((ITERS + 1, rows, GRID * GRID), jnp.int32),
            pltpu.VMEM((2, 2, wide, wide), jnp.bfloat16),
            pltpu.VMEM((2, 2, 2 * GRID, 2 * GRID), jnp.bfloat16),
            pltpu.VMEM((2 * ROUGH, LANES), jnp.float32),
            pltpu.VMEM((6, rows, GRID * GRID), jnp.float32),
            pltpu.VMEM((6, 2, ROUGH, rows, LANES), jnp.float32),
            pltpu.VMEM((6, 2, own_lines, GRID, LANES), jnp.float32),
            pltpu.VMEM((6, 2, own_lines, GRID, LANES), jnp.float32),
            pltpu.VMEM((6, 2, ROUGH, rows, LANES), jnp.float32),
            pltpu.VMEM((2 * GRID, 6 * LANES), jnp.float32),
            pltpu.VMEM((STATS, 8, LANES), jnp.float32),
            pltpu.VMEM((slabs, STATS, LANES), jnp.float32),
            pltpu.VMEM((points, STATS, LANES), jnp.float32),
            pltpu.SemaphoreType.DMA((8,)),
            pltpu.SemaphoreType.DMA((2, rows // 8, slabs - 1, own_lines)),
            pltpu.SemaphoreType.DMA((2, rows // 8, slabs - 1, own_lines)),
            pltpu.SemaphoreType.DMA((slabs - 1,)),
            pltpu.SemaphoreType.DMA((slabs - 1,)),
            pltpu.SemaphoreType.DMA((points - 1,)),
            pltpu.SemaphoreType.DMA((points - 1,)),
        ],
        compiler_params=pltpu.CompilerParams(
            collective_id=0, has_side_effects=True, vmem_limit_bytes=40 * 1024 * 1024
        ),
    )(
        macro_strain,
        phase_ids,
        yield_flags[0],
        plastic_strain[0],
        jnp.asarray(np.stack([host_halves(depth), host_halves(depth_back)])),
        jnp.asarray(np.stack([host_halves(line), host_halves(line_back)])),
        twiddle_table().reshape(2 * ROUGH, LANES),
    )
    means = stats[:, :, 0] / float(GRID**3)
    mean_stress = means[:, :6]
    pair_place = np.zeros((6, 6), np.int32)
    place = 7
    for a in range(6):
        for b in range(a, 6):
            pair_place[a, b] = pair_place[b, a] = place
            place += 1
    outer = jnp.stack([means[:, place] for place in pair_place.reshape(-1)], axis=1)
    outer = outer.reshape(points, 6, 6)
    tangent = jax.vmap(tangent_matrix)(means[:, 6], outer)
    weights = np.asarray(PAIR_WEIGHTS)
    weighted = lookup * weights[None, :, None] * QUADRATURE_WEIGHT
    weighted = jnp.asarray(weighted.reshape(48, 24), jnp.float32)
    element_force = jnp.sum(
        mean_stress.reshape(element_count, 48, 1) * weighted[None], axis=1
    )
    best = lax.Precision.HIGHEST
    spread = jnp.einsum(
        "equn,qnv->equv",
        tangent.reshape(element_count, 8, 6, 6),
        jnp.asarray(lookup, jnp.float32),
        precision=best,
    ).reshape(element_count, 48, 24)
    element_stiffness = jnp.einsum("rh,erv->ehv", weighted, spread, precision=best)
    forces = jnp.einsum(
        "eck,ecn->nk", element_force.reshape(element_count, 8, 3), placing, precision=best
    )
    block = element_stiffness.reshape(element_count, 8, 3, 8, 3)
    stiffness = jnp.einsum("ecn,eckdl,edm->nkml", placing, block, placing, precision=best)
    stiffness = stiffness.reshape(3 * node_count, 3 * node_count)
    own_stress = lax.dynamic_slice(mean_stress, (point, 0), (1, 6))
    own_tangent = lax.dynamic_slice(tangent, (point, 0, 0), (1, 6, 6))
    return (own_stress, own_tangent, forces, stiffness)


def solution(mesh):
    slabs = mesh.shape["slab"]
    fits = slabs > 1 and ROUGH % slabs == 0 and GRID // slabs % 16 == 0
    body = fused_on_device if fits else on_device
    return jax.shard_map(
        body,
        mesh=mesh,
        in_specs=(
            P("slab", None),
            P("rve", None, "slab", None),
            P("rve", None, "slab", None),
            P(),
            P(),
        ),
        out_specs=(P("rve", None), P("rve", None, None), P(), P()),
        check_vma=False,
    )
```

```python
import math

import jax
import jax.numpy as jnp
import numpy as np
from jax import lax
from jax.experimental import pallas as pl
from jax.experimental.pallas import tpu as pltpu
from jax.sharding import PartitionSpec as P

GRID = 64
ITERS = 2


SHEAR_MODULUS = 80.0
BULK_MODULUS = 160.0
REFERENCE_SHEAR = 80.0
REFERENCE_LAME = 160.0 - 160.0 / 3.0
TANGENT_UNIT = 100.0
QUADRATURE_WEIGHT = 0.125
DIAGONAL_PART = (1.0, 1.0, 1.0, 0.0, 0.0, 0.0)
PAIR_WEIGHTS = (1.0, 1.0, 1.0, 2.0, 2.0, 2.0)
TENSOR_PAIRS = ((0, 0), (1, 1), (2, 2), (1, 2), (0, 2), (0, 1))
TENSOR_ROWS = ((0, 5, 4), (5, 1, 3), (4, 3, 2))


def gradient_table():
    inverse_root = 1.0 / math.sqrt(3.0)
    table_rows = np.zeros((8, 6, 24))
    for gauss_corner in range(8):
        position = [
            0.5 + (2 * (gauss_corner >> axis_number & 1) - 1) * 0.5 * inverse_root
            for axis_number in range(3)
        ]
        for corner in range(8):
            corner_bits = [corner >> axis_number & 1 for axis_number in range(3)]
            factors = [
                position[axis_number] * corner_bits[axis_number]
                + (1.0 - position[axis_number]) * (1 - corner_bits[axis_number])
                for axis_number in range(3)
            ]
            slopes = []
            for axis_number in range(3):
                slope_value = 2.0 * corner_bits[axis_number] - 1.0
                for other_axis in range(3):
                    if other_axis != axis_number:
                        slope_value = slope_value * factors[other_axis]
                slopes.append(slope_value)
            column = 3 * corner
            table_rows[gauss_corner, 0, column] += slopes[0]
            table_rows[gauss_corner, 1, column + 1] += slopes[1]
            table_rows[gauss_corner, 2, column + 2] += slopes[2]
            table_rows[gauss_corner, 3, column + 1] += 0.5 * slopes[2]
            table_rows[gauss_corner, 3, column + 2] += 0.5 * slopes[1]
            table_rows[gauss_corner, 4, column] += 0.5 * slopes[2]
            table_rows[gauss_corner, 4, column + 2] += 0.5 * slopes[0]
            table_rows[gauss_corner, 5, column] += 0.5 * slopes[1]
            table_rows[gauss_corner, 5, column + 1] += 0.5 * slopes[0]
    return table_rows


def point_geometry(points, connectivity, corner_lookup, node_count):
    element_count = connectivity.shape[0]
    point_count = points.shape[0]
    corner_selector = (points[:, None] % 8 == jnp.arange(8, dtype=jnp.int32)[None, :]).astype(
        jnp.float32
    )
    strain_row_values = jnp.einsum(
        "zu,utf->ztf", corner_selector, corner_lookup, precision=lax.Precision.HIGHEST
    )
    element_onehot = points[:, None] // 8 == jnp.arange(element_count, dtype=jnp.int32)[None, :]
    corner_nodes = jnp.sum(
        jnp.where(element_onehot[:, :, None], connectivity[None, :, :], 0), axis=1
    )
    degrees = 3 * corner_nodes[:, :, None] + jnp.arange(3, dtype=jnp.int32)[None, None, :]
    degrees = degrees.reshape(point_count, 24)
    placing = (
        degrees[:, :, None] == jnp.arange(3 * node_count, dtype=jnp.int32)[None, None, :]
    ).astype(jnp.float32)
    return (strain_row_values, placing)


def macro_strains(strain_row_values, placing, displacements):
    nodal_quantities = jnp.einsum(
        "gpn,n->gp", placing, displacements.reshape(-1), precision=lax.Precision.HIGHEST
    )
    return jnp.einsum(
        "vxw,vw->vx", strain_row_values, nodal_quantities, precision=lax.Precision.HIGHEST
    )


def material_response(strain, plastic, phase_ids, flag_values):
    diagonal = jnp.asarray(DIAGONAL_PART, jnp.float32)[:, None]
    weights = jnp.asarray(PAIR_WEIGHTS, jnp.float32)[:, None]
    martensite = phase_ids == 1
    yield_stress = jnp.where(martensite, 1.2, 0.3).astype(jnp.float32)
    hardening = jnp.where(martensite, 10.0, 2.0).astype(jnp.float32)
    elastic = strain - plastic
    volume = elastic[0] + elastic[1] + elastic[2]
    trial_dev = 2.0 * SHEAR_MODULUS * (elastic - diagonal * (volume / 3.0))
    equivalent = jnp.sqrt(1.5 * jnp.sum(weights * trial_dev * trial_dev, axis=0))
    bounded = jnp.maximum(equivalent, yield_stress)
    return_ratio = 3.0 * SHEAR_MODULUS / (3.0 * SHEAR_MODULUS + hardening)
    active = flag_values.astype(jnp.float32)
    plastic_flow = active * (equivalent - yield_stress) / bounded
    softening = 1.0 - return_ratio * plastic_flow
    stress = trial_dev * softening + diagonal * (BULK_MODULUS * volume)
    shear_term = 2.0 * SHEAR_MODULUS * softening
    tangent_weight = (
        3.0 * SHEAR_MODULUS * return_ratio * active * yield_stress / (bounded * bounded * bounded)
    )
    return (stress, trial_dev, shear_term, tangent_weight)


def wave_terms(index_x, index_y, index_z):
    middle = GRID // 2
    signed = []
    for indices in (index_x, index_y, index_z):
        wrapped = jnp.where(indices < middle, indices, indices - GRID)
        signed.append(jnp.where(indices == middle, 0, wrapped))
    nyquist_free = (index_x != middle) & (index_y != middle) & (index_z != middle)
    length = signed[0] * signed[0] + signed[1] * signed[1] + signed[2] * signed[2]
    keep_mask = (nyquist_free & (length > 0)).astype(jnp.float32)
    inverse_length = 1.0 / jnp.sqrt(jnp.maximum(length, 1).astype(jnp.float32))
    normals = [signed_entry.astype(jnp.float32) * inverse_length for signed_entry in signed]
    return (normals, keep_mask)


def project_green(components, normals, keep_mask):
    traction = [
        components[tensor_row[0]] * normals[0]
        + components[tensor_row[1]] * normals[1]
        + components[tensor_row[2]] * normals[2]
        for tensor_row in TENSOR_ROWS
    ]
    normal_load = normals[0] * traction[0] + normals[1] * traction[1] + normals[2] * traction[2]
    coupling = (REFERENCE_LAME + REFERENCE_SHEAR) / (
        REFERENCE_SHEAR * (REFERENCE_LAME + 2.0 * REFERENCE_SHEAR)
    )
    result_list = []
    for left_axis, right_axis in TENSOR_PAIRS:
        entry_value = (
            normals[left_axis] * traction[right_axis] + normals[right_axis] * traction[left_axis]
        ) / (2.0 * REFERENCE_SHEAR)
        entry_value = (
            entry_value - coupling * normals[left_axis] * normals[right_axis] * normal_load
        )
        result_list.append(entry_value * keep_mask)
    return jnp.stack(result_list)


def tangent_matrix(mean_shear, outer_sum):
    diagonal = jnp.asarray(DIAGONAL_PART, jnp.float32)
    volumetric = diagonal[:, None] * diagonal[None, :]
    weights = jnp.asarray(PAIR_WEIGHTS, jnp.float32)
    identity = jnp.eye(6, dtype=jnp.float32)
    whole = (
        BULK_MODULUS * volumetric
        + mean_shear * (identity - volumetric / 3.0)
        - outer_sum * weights[None, :]
    )
    return whole / TANGENT_UNIT


def assemble(stress_values, tangent_moduli, strain_row_values, placing):
    weights = jnp.asarray(PAIR_WEIGHTS, jnp.float32)
    force_row_values = strain_row_values * weights[None, :, None]
    element_force_vector = QUADRATURE_WEIGHT * jnp.einsum(
        "mbh,mb->mh", force_row_values, stress_values, precision=lax.Precision.HIGHEST
    )
    element_stiffness_matrix = QUADRATURE_WEIGHT * jnp.einsum(
        "xoh,xon,xnv->xhv",
        force_row_values,
        tangent_moduli,
        strain_row_values,
        precision=lax.Precision.HIGHEST,
    )
    forces = jnp.einsum("gp,gpn->n", element_force_vector, placing, precision=lax.Precision.HIGHEST)
    stiffness = jnp.einsum(
        "gpq,gpm,gqn->mn",
        element_stiffness_matrix,
        placing,
        placing,
        precision=lax.Precision.HIGHEST,
    )
    return (forces.reshape(-1, 3), stiffness)


def angle_table(count_rows, count_cols):
    rows_index = lax.broadcasted_iota(jnp.int32, (count_rows, count_cols), 0)
    cols_index = lax.broadcasted_iota(jnp.int32, (count_rows, count_cols), 1)
    angles = 2.0 * math.pi / GRID * (rows_index * cols_index % GRID).astype(jnp.float32)
    return (jnp.cos(angles), jnp.sin(angles))


def complex_table(inverse):
    cosine, sine = angle_table(GRID, GRID)
    if inverse:
        first_row = jnp.stack([cosine, -sine], axis=1)
        second_row = jnp.stack([sine, cosine], axis=1)
    else:
        first_row = jnp.stack([cosine, sine], axis=1)
        second_row = jnp.stack([-sine, cosine], axis=1)
    return jnp.stack([first_row, second_row], axis=0)


def on_device(phase_ids, yield_flags, plastic_strain, displacements, connectivity):
    slabs = lax.axis_size("slab")
    slab_index = lax.axis_index("slab")
    plane_count = phase_ids.shape[0]
    row_planes = GRID // slabs
    node_count = displacements.shape[0]
    corner_lookup = jnp.asarray(gradient_table(), jnp.float32)
    gauss_point = lax.axis_index("rve")
    own_points = jnp.full((1,), gauss_point, jnp.int32)
    strain_row_values, placing = point_geometry(own_points, connectivity, corner_lookup, node_count)
    macro_strain = macro_strains(strain_row_values, placing, displacements)[0]
    phases = phase_ids.reshape(-1)
    plastic = plastic_strain[0].reshape(6, -1)
    point_flags = yield_flags[0]
    columns = GRID // 2
    kept_index = lax.broadcasted_iota(jnp.int32, (columns, 1), 0)
    column_weight = jnp.where(kept_index == 0, 1.0, 2.0).astype(jnp.float32)
    depth_cos, depth_sin = angle_table(columns, GRID)
    forward_depth = jnp.stack([depth_cos, -depth_sin], axis=0)
    inverse_depth = jnp.stack(
        [column_weight * depth_cos, -column_weight * depth_sin], axis=0
    ) / float(GRID**3)
    forward_plane = complex_table(False)
    inverse_plane = complex_table(True)
    index_x = lax.broadcasted_iota(jnp.int32, (GRID, 1, 1), 0)
    index_y = slab_index * row_planes + lax.broadcasted_iota(jnp.int32, (1, row_planes, 1), 1)
    index_z = lax.broadcasted_iota(jnp.int32, (1, 1, columns), 2)
    normals, keep_mask = wave_terms(index_x, index_y, index_z)
    strain = jnp.broadcast_to(macro_strain[:, None], plastic.shape)
    for iteration in range(ITERS):
        stress = material_response(strain, plastic, phases, point_flags[iteration].reshape(-1))[0]
        voxel_block = stress.reshape(6, plane_count, GRID, GRID)
        spectral = jnp.einsum(
            "pkz,cxyz->pcxyk", forward_depth, voxel_block, precision=lax.Precision.HIGHEST
        )
        spectral = jnp.einsum(
            "pjqy,qcxyk->pcxjk", forward_plane, spectral, precision=lax.Precision.HIGHEST
        )
        spectral = lax.all_to_all(spectral, "slab", split_axis=3, concat_axis=2, tiled=True)
        spectral = jnp.einsum(
            "pjqx,qcxyk->pcjyk", forward_plane, spectral, precision=lax.Precision.HIGHEST
        )
        projected = project_green(
            [spectral[:, component] for component in range(6)], normals, keep_mask
        )
        spectral = jnp.einsum(
            "pjqx,cqxyk->pcjyk", inverse_plane, projected, precision=lax.Precision.HIGHEST
        )
        spectral = lax.all_to_all(spectral, "slab", split_axis=2, concat_axis=3, tiled=True)
        spectral = jnp.einsum(
            "pjqy,qcxyk->pcxjk", inverse_plane, spectral, precision=lax.Precision.HIGHEST
        )
        correction = jnp.einsum(
            "pkz,pcxyk->cxyz", inverse_depth, spectral, precision=lax.Precision.HIGHEST
        )
        strain = strain - correction.reshape(6, -1)
    stress, trial_dev, shear_term, tangent_weight = material_response(
        strain, plastic, phases, point_flags[ITERS].reshape(-1)
    )
    outer_part = jnp.dot(
        trial_dev * tangent_weight[None, :], trial_dev.T, precision=lax.Precision.HIGHEST
    )
    stress_total, shear_total, outer_total = lax.psum(
        (jnp.sum(stress, axis=1), jnp.sum(shear_term), outer_part), "slab"
    )
    voxel_count = float(GRID**3)
    mean_stress = stress_total / voxel_count
    tangent = tangent_matrix(shear_total / voxel_count, outer_total / voxel_count)
    own_forces, own_stiffness = assemble(
        mean_stress[None], tangent[None], strain_row_values, placing
    )
    forces, stiffness = lax.psum((own_forces, own_stiffness), "rve")
    return (mean_stress[None], tangent[None], forces, stiffness)


ROUGH = 16
GROUPS = 4
LANES = 128
STATS = 32
MESH = pl.DeviceIdType.MESH


def halves(value):
    high = value.astype(jnp.bfloat16)
    return high, (value - high.astype(jnp.float32)).astype(jnp.bfloat16)


def mul(left, right):
    return jnp.dot(left, right, preferred_element_type=jnp.float32)


def host_halves(table):
    table = np.asarray(table, np.float32)
    high = table.astype(jnp.bfloat16)
    low = (table - high.astype(np.float32)).astype(jnp.bfloat16)
    return np.stack([high, low])


def depth_tables():
    kept = GRID // 2
    angles = 2.0 * np.pi / GRID * (np.arange(GRID)[:, None] * np.arange(kept)[None, :] % GRID)
    weight = np.where(np.arange(kept) == 0, 1.0, 2.0) / float(GRID**3)
    eye = np.eye(GROUPS)
    forward = np.concatenate([np.kron(eye, np.cos(angles)), np.kron(eye, -np.sin(angles))], axis=1)
    back_cos = (np.cos(angles) * weight[None, :]).T
    back_sin = (-np.sin(angles) * weight[None, :]).T
    inverse = np.concatenate([np.kron(eye, back_cos), np.kron(eye, back_sin)], axis=0)
    return forward, inverse


def line_tables():
    angles = 2.0 * np.pi / GRID * (np.arange(GRID)[:, None] * np.arange(GRID)[None, :] % GRID)
    cosine, sine = np.cos(angles), np.sin(angles)
    forward = np.block([[cosine, sine], [-sine, cosine]])
    inverse = np.block([[cosine, -sine], [sine, cosine]])
    return forward, inverse


def twiddle_table():
    lane_group = np.arange(LANES) // (LANES // GROUPS)
    angles = 2.0 * np.pi / GRID * (np.arange(ROUGH)[:, None] * lane_group[None, :])
    return jnp.asarray(np.stack([np.cos(angles), -np.sin(angles)], axis=1), jnp.float32)


def four_point(re, im, sign):
    a_re, a_im = re[0] + re[2], im[0] + im[2]
    b_re, b_im = re[0] - re[2], im[0] - im[2]
    c_re, c_im = re[1] + re[3], im[1] + im[3]
    d_re, d_im = re[1] - re[3], im[1] - im[3]
    e_re, e_im = (d_im, -d_re) if sign < 0 else (-d_im, d_re)
    return (
        [a_re + c_re, b_re + e_re, a_re - c_re, b_re - e_re],
        [a_im + c_im, b_im + e_im, a_im - c_im, b_im - e_im],
    )


def sixteen_point(re, im, sign):
    inner_re, inner_im = [], []
    for b in range(4):
        part_re, part_im = four_point(re[b::4], im[b::4], sign)
        for ka in range(1, 4):
            if b:
                angle = 2.0 * math.pi * b * ka / 16.0
                cosine, sine = math.cos(angle), sign * math.sin(angle)
                old_re, old_im = part_re[ka], part_im[ka]
                part_re[ka] = old_re * cosine - old_im * sine
                part_im[ka] = old_re * sine + old_im * cosine
        inner_re.append(part_re)
        inner_im.append(part_im)
    out_re, out_im = [None] * 16, [None] * 16
    for ka in range(4):
        part_re, part_im = four_point(
            [inner_re[b][ka] for b in range(4)], [inner_im[b][ka] for b in range(4)], sign
        )
        for kb in range(4):
            out_re[ka + 4 * kb] = part_re[kb]
            out_im[ka + 4 * kb] = part_im[kb]
    return out_re, out_im


def voxel_law(elastic, phase, flag, want_tangent):
    martensite = phase == 1
    yield_stress = jnp.where(martensite, 1.2, 0.3).astype(jnp.float32)
    base = 3.0 * SHEAR_MODULUS
    ratio = jnp.where(martensite, base / (base + 10.0), base / (base + 2.0)).astype(jnp.float32)
    volume = elastic[0] + elastic[1] + elastic[2]
    third = volume * (1.0 / 3.0)
    trial = [
        (2.0 * SHEAR_MODULUS) * (elastic[n] - third if n < 3 else elastic[n]) for n in range(6)
    ]
    square = [value * value for value in trial]
    norm = square[0] + square[1] + square[2] + 2.0 * (square[3] + square[4] + square[5])
    equivalent = jnp.sqrt(1.5 * norm)
    bounded = jnp.maximum(equivalent, yield_stress)
    active = flag.astype(jnp.float32)
    inverse = 1.0 / bounded
    active_ratio = active * ratio
    softening = 1.0 - active_ratio * ((equivalent - yield_stress) * inverse)
    pressure = BULK_MODULUS * volume
    stress = [trial[n] * softening + pressure if n < 3 else trial[n] * softening for n in range(6)]
    if not want_tangent:
        return stress
    beta = base * active_ratio * yield_stress * (inverse * inverse * inverse)
    return stress, trial, (2.0 * SHEAR_MODULUS) * softening, beta


def cell_kernel(
    slabs, points, macro_ref, phase_hbm, flag_hbm, plastic_hbm, depth_hbm, line_hbm, twiddle_hbm,
    out_ref,
    phase_ref, flag_ref, depth_ref, line_ref, twiddle_ref,
    elastic, planes, lines, lines_back, planes_back, work, sums, slab_sums, point_sums,
    load_sem, send_sem, recv_sem, slab_send, slab_recv, point_send, point_recv,
):
    slab = lax.axis_index("slab")
    point = lax.axis_index("rve")
    rows = GRID // slabs
    own_lines = ROUGH // slabs
    wide = GROUPS * GRID

    barrier = pltpu.get_barrier_semaphore()
    for step in range(1, slabs):
        pl.semaphore_signal(
            barrier, inc=1, device_id={"slab": lax.rem(slab + step, slabs)}, device_id_type=MESH
        )
    for step in range(1, points):
        pl.semaphore_signal(
            barrier, inc=1, device_id={"rve": lax.rem(point + step, points)}, device_id_type=MESH
        )

    def lane_block(index):
        return pl.ds(pl.multiple_of(index * wide, wide), wide)

    def row_block(index):
        return pl.ds(pl.multiple_of(index * rows, rows), rows)

    parts = rows // 8

    def part_rows(part):
        return pl.ds(pl.multiple_of(part * 8, 8), 8)

    pairs = [
        (plastic_hbm.at[:, 0:8], elastic.at[:, 0:8]),
        (phase_hbm, phase_ref),
        (flag_hbm.at[0], flag_ref.at[0]),
        (depth_hbm, depth_ref),
        (twiddle_hbm, twiddle_ref),
        (plastic_hbm.at[:, 8:rows], elastic.at[:, 8:rows]),
        (line_hbm, line_ref),
        (flag_hbm.at[1:], flag_ref.at[1:]),
    ]
    loads = [
        pltpu.make_async_copy(source, target, load_sem.at[place])
        for place, (source, target) in enumerate(pairs)
    ]
    for load in loads:
        load.start()

    lane = lax.broadcasted_iota(jnp.int32, (1, LANES), 1)
    group = lane >> 5
    high_sign = jnp.where((group >> 1) == 0, 1.0, -1.0).astype(jnp.float32)
    low_sign = jnp.where((group & 1) == 0, 1.0, -1.0).astype(jnp.float32)
    low_first = (group & 1) == 0
    corner = group == 3

    def across_high(value):
        return pltpu.roll(value, 64, 1) + high_sign * value

    def across_low(value):
        partner = jnp.where(low_first, pltpu.roll(value, 96, 1), pltpu.roll(value, 32, 1))
        return partner + low_sign * value

    def groups_forward(re, im, cosine, sine):
        re, im = re * cosine - im * sine, re * sine + im * cosine
        re, im = across_high(re), across_high(im)
        re, im = jnp.where(corner, im, re), jnp.where(corner, -re, im)
        return across_low(re), across_low(im)

    def groups_back(re, im, cosine, sine):
        re, im = across_low(re), across_low(im)
        re, im = jnp.where(corner, -im, re), jnp.where(corner, re, im)
        re, im = across_high(re), across_high(im)
        return re * cosine + im * sine, im * cosine - re * sine

    def sixteen(ref, sign, part):
        @pl.loop(0, 6)
        def _(n):
            picked = part_rows(part)
            re = [ref[n, 0, k, picked, :] for k in range(ROUGH)]
            im = [ref[n, 1, k, picked, :] for k in range(ROUGH)]
            re, im = sixteen_point(re, im, sign)
            for k in range(ROUGH):
                ref[n, 0, k, picked, :] = re[k]
                ref[n, 1, k, picked, :] = im[k]

    def slab_rows(index, part):
        return pl.ds(pl.multiple_of(index * rows + part * 8, 8), 8)

    def forward_copy(step, chunk, part, target, source):
        return pltpu.make_async_remote_copy(
            src_ref=planes.at[:, :, target * own_lines + chunk, part_rows(part), :],
            dst_ref=lines.at[:, :, chunk, slab_rows(source, part), :],
            send_sem=send_sem.at[0, part, step - 1, chunk],
            recv_sem=recv_sem.at[0, part, step - 1, chunk],
            device_id={"slab": target},
            device_id_type=MESH,
        )

    def back_copy(step, chunk, part, target, source):
        return pltpu.make_async_remote_copy(
            src_ref=lines_back.at[:, :, chunk, slab_rows(target, part), :],
            dst_ref=planes_back.at[:, :, source * own_lines + chunk, part_rows(part), :],
            send_sem=send_sem.at[1, part, step - 1, chunk],
            recv_sem=recv_sem.at[1, part, step - 1, chunk],
            device_id={"slab": target},
            device_id_type=MESH,
        )

    def to(step):
        return lax.rem(slab + step, slabs)

    def come_from(step):
        return lax.rem(slab + slabs - step, slabs)

    coupling = (REFERENCE_LAME + REFERENCE_SHEAR) / (
        REFERENCE_SHEAR * (REFERENCE_LAME + 2.0 * REFERENCE_SHEAR)
    )
    middle = GRID // 2

    def signed(index):
        wrapped = jnp.where(index < middle, index, index - GRID)
        return jnp.where(index == middle, 0, wrapped)

    def line_stage(chunk):
        stacked = jnp.concatenate(
            [lines[n, :, chunk].reshape(2 * GRID, LANES) for n in range(6)], axis=1
        )
        high, low = halves(stacked)
        work[...] = mul(line_ref[0, 0], high) + mul(line_ref[0, 0], low) + mul(line_ref[0, 1], high)
        index_y = slab * own_lines + chunk + ROUGH * ((group >> 1) + 2 * (group & 1))
        index_z = lane & (LANES // GROUPS - 1)
        freq_y = signed(index_y)
        freq_z = index_z

        @pl.loop(0, GRID // 8)
        def _(block):
            index_x = block * 8 + lax.broadcasted_iota(jnp.int32, (8, 1), 0)
            freq_x = signed(index_x)
            length = freq_x * freq_x + (freq_y * freq_y + freq_z * freq_z)
            keep = (index_x != middle) & (index_y != middle) & (length > 0)
            inverse = jnp.where(keep, 1.0 / jnp.maximum(length, 1).astype(jnp.float32), 0.0)
            scale = inverse * (1.0 / REFERENCE_SHEAR)
            along = coupling * inverse * inverse
            xi = [freq.astype(jnp.float32) for freq in (freq_x, freq_y, freq_z)]
            for part in range(2):
                picked = pl.ds(pl.multiple_of(part * GRID + block * 8, 8), 8)
                tau = [work[picked, n * LANES : (n + 1) * LANES] for n in range(6)]
                load = [
                    tau[row[0]] * xi[0] + tau[row[1]] * xi[1] + tau[row[2]] * xi[2]
                    for row in TENSOR_ROWS
                ]
                normal = (xi[0] * load[0] + xi[1] * load[1] + xi[2] * load[2]) * along
                field = [0.5 * (load[d] * scale - xi[d] * normal) for d in range(3)]
                for n, (left, right) in enumerate(TENSOR_PAIRS):
                    value = xi[left] * field[right] + xi[right] * field[left]
                    work[picked, n * LANES : (n + 1) * LANES] = value

        high, low = halves(work[...])
        result = (
            mul(line_ref[1, 0], high) + mul(line_ref[1, 0], low) + mul(line_ref[1, 1], high)
        )
        for n in range(6):
            lines_back[n, :, chunk] = result[:, n * LANES : (n + 1) * LANES].reshape(
                2, GRID, LANES
            )

    def twiddles(line):
        return twiddle_ref[pl.ds(2 * line, 1), :], twiddle_ref[pl.ds(2 * line + 1, 1), :]

    def plane_forward(iteration, part):
        picked = part_rows(part)

        @pl.loop(0, ROUGH // 4)
        def _(batch):
            pieces = []
            for inner in range(4):
                at = lane_block(batch * 4 + inner)
                pieces += voxel_law(
                    [elastic[n, picked, at] for n in range(6)],
                    phase_ref[picked, at],
                    flag_ref[iteration, picked, at],
                    False,
                )
            high, low = halves(jnp.concatenate(pieces, axis=0))
            result = (
                mul(high, depth_ref[0, 0]) + mul(low, depth_ref[0, 0]) + mul(high, depth_ref[0, 1])
            )
            for inner in range(4):
                for n in range(6):
                    first = (inner * 6 + n) * 8
                    planes[n, 0, batch * 4 + inner, picked, :] = result[first : first + 8, :LANES]
                    planes[n, 1, batch * 4 + inner, picked, :] = result[first : first + 8, LANES:]

        sixteen(planes, -1, part)

        @pl.loop(0, own_lines)
        def _(chunk):
            for step in list(range(1, slabs)) + [0]:
                target = to(step)
                line = target * own_lines + chunk
                cosine, sine = twiddles(line)
                for n in range(6):
                    re, im = groups_forward(
                        planes[n, 0, line, picked, :], planes[n, 1, line, picked, :], cosine, sine
                    )
                    if step:
                        planes[n, 0, line, picked, :] = re
                        planes[n, 1, line, picked, :] = im
                    else:
                        lines[n, 0, chunk, slab_rows(slab, part), :] = re
                        lines[n, 1, chunk, slab_rows(slab, part), :] = im
                if step:
                    forward_copy(step, chunk, part, target, slab).start()

    def plane_back(part):
        picked = part_rows(part)

        @pl.loop(0, own_lines)
        def _(chunk):
            for step in range(slabs):
                source = come_from(step)
                line = source * own_lines + chunk
                if step:
                    back_copy(step, chunk, part, to(step), source).wait_recv()
                cosine, sine = twiddles(line)
                for n in range(6):
                    if step:
                        re = planes_back[n, 0, line, picked, :]
                        im = planes_back[n, 1, line, picked, :]
                    else:
                        re = lines_back[n, 0, chunk, slab_rows(slab, part), :]
                        im = lines_back[n, 1, chunk, slab_rows(slab, part), :]
                    re, im = groups_back(re, im, cosine, sine)
                    planes_back[n, 0, line, picked, :] = re
                    planes_back[n, 1, line, picked, :] = im

        sixteen(planes_back, 1, part)

        @pl.loop(0, ROUGH // 4)
        def _(batch):
            stacked = jnp.concatenate(
                [
                    jnp.concatenate(
                        [
                            planes_back[n, side, batch * 4 + inner, picked, :]
                            for inner in range(4)
                            for n in range(6)
                        ],
                        axis=0,
                    )
                    for side in range(2)
                ],
                axis=1,
            )
            high, low = halves(stacked)
            result = (
                mul(high, depth_ref[1, 0]) + mul(low, depth_ref[1, 0]) + mul(high, depth_ref[1, 1])
            )
            for inner in range(4):
                at = lane_block(batch * 4 + inner)
                for n in range(6):
                    first = (inner * 6 + n) * 8
                    elastic[n, picked, at] = elastic[n, picked, at] - result[first : first + 8]

    def final_sums(part):
        picked = part_rows(part)

        @pl.loop(0, ROUGH)
        def _(block):
            at = lane_block(block)
            stress, trial, shear, beta = voxel_law(
                [elastic[n, picked, at] for n in range(6)],
                phase_ref[picked, at],
                flag_ref[ITERS, picked, at],
                True,
            )
            entries = stress + [shear]
            for a in range(6):
                weighted = beta * trial[a]
                for b in range(a, 6):
                    entries.append(weighted * trial[b])
            for place, value in enumerate(entries):
                sums[place] = sums[place] + (value[:, :LANES] + value[:, LANES:])

    sums[...] = jnp.zeros_like(sums)
    for load in loads[:5]:
        load.wait()

    @pl.loop(0, parts)
    def _(part):
        @pl.when(part == 1)
        def _():
            loads[5].wait()

        picked = part_rows(part)

        @pl.loop(0, ROUGH)
        def _(block):
            at = lane_block(block)
            for n in range(6):
                elastic[n, picked, at] = macro_ref[n] - elastic[n, picked, at]

        @pl.when(part == 0)
        def _():
            pl.semaphore_wait(barrier, slabs - 1 + points - 1)

        plane_forward(0, part)

    for load in loads[6:]:
        load.wait()

    @pl.loop(0, ITERS)
    def _(iteration):
        @pl.loop(0, own_lines)
        def _(chunk):
            for step in range(1, slabs):
                for part in range(parts):
                    forward_copy(step, chunk, part, to(step), come_from(step)).wait_recv()
            line_stage(chunk)
            for step in range(1, slabs):
                back_copy(step, chunk, 0, to(step), slab).start()

        @pl.loop(0, own_lines)
        def _(chunk):
            for part in range(1, parts):
                for step in range(1, slabs):
                    back_copy(step, chunk, part, to(step), slab).start()

        @pl.loop(0, parts)
        def _(part):
            plane_back(part)

            @pl.loop(0, own_lines)
            def _(chunk):
                for step in range(1, slabs):
                    forward_copy(step, chunk, part, to(step), slab).wait_send()
                    back_copy(step, chunk, part, to(step), slab).wait_send()

            @pl.when(iteration < ITERS - 1)
            def _():
                plane_forward(iteration + 1, part)

            @pl.when(iteration == ITERS - 1)
            def _():
                final_sums(part)

    slab_sums[slab] = jnp.sum(sums[...], axis=1)

    def slab_copy(step, source):
        return pltpu.make_async_remote_copy(
            src_ref=slab_sums.at[source],
            dst_ref=slab_sums.at[source],
            send_sem=slab_send.at[step - 1],
            recv_sem=slab_recv.at[step - 1],
            device_id={"slab": to(step)},
            device_id_type=MESH,
        )

    def point_copy(step, source):
        return pltpu.make_async_remote_copy(
            src_ref=point_sums.at[source],
            dst_ref=point_sums.at[source],
            send_sem=point_send.at[step - 1],
            recv_sem=point_recv.at[step - 1],
            device_id={"rve": lax.rem(point + step, points)},
            device_id_type=MESH,
        )

    for step in range(1, slabs):
        slab_copy(step, slab).start()
    for step in range(1, slabs):
        slab_copy(step, come_from(step)).wait_recv()
    total = slab_sums[0]
    for other in range(1, slabs):
        total = total + slab_sums[other]
    point_sums[point] = jnp.broadcast_to(
        jnp.sum(total, axis=1, keepdims=True), (STATS, LANES)
    )
    for step in range(1, points):
        point_copy(step, point).start()
    for step in range(1, points):
        point_copy(step, lax.rem(point + points - step, points)).wait_recv()
    out_ref[...] = point_sums[...]
    for step in range(1, slabs):
        slab_copy(step, slab).wait_send()
    for step in range(1, points):
        point_copy(step, point).wait_send()


def fused_on_device(phase_ids, yield_flags, plastic_strain, displacements, connectivity):
    slabs = lax.axis_size("slab")
    points = lax.axis_size("rve")
    rows = phase_ids.shape[0]
    node_count = displacements.shape[0]
    element_count = connectivity.shape[0]
    own_lines = ROUGH // slabs
    point = lax.axis_index("rve")
    lookup = gradient_table()
    placing = (
        connectivity[:, :, None] == jnp.arange(node_count, dtype=jnp.int32)[None, None, :]
    ).astype(jnp.float32)
    corner_moves = jnp.sum(placing[:, :, :, None] * displacements[None, None, :, :], axis=2)
    all_strain = jnp.sum(
        jnp.asarray(lookup, jnp.float32)[None] * corner_moves.reshape(element_count, 1, 1, 24),
        axis=3,
    ).reshape(points, 6)
    macro_strain = lax.dynamic_slice(all_strain, (point, 0), (1, 6))[0]

    depth, depth_back = depth_tables()
    line, line_back = line_tables()
    wide = GROUPS * GRID
    vmem = pl.BlockSpec(memory_space=pltpu.VMEM)
    stats = pl.pallas_call(
        lambda *refs: cell_kernel(slabs, points, *refs),
        out_shape=jax.ShapeDtypeStruct((points, STATS, LANES), jnp.float32),
        in_specs=[pl.BlockSpec(memory_space=pltpu.SMEM)]
        + [pl.BlockSpec(memory_space=pltpu.HBM)] * 6,
        out_specs=vmem,
        scratch_shapes=[
            pltpu.VMEM((rows, GRID * GRID), jnp.int32),
            pltpu.VMEM((ITERS + 1, rows, GRID * GRID), jnp.int32),
            pltpu.VMEM((2, 2, wide, wide), jnp.bfloat16),
            pltpu.VMEM((2, 2, 2 * GRID, 2 * GRID), jnp.bfloat16),
            pltpu.VMEM((2 * ROUGH, LANES), jnp.float32),
            pltpu.VMEM((6, rows, GRID * GRID), jnp.float32),
            pltpu.VMEM((6, 2, ROUGH, rows, LANES), jnp.float32),
            pltpu.VMEM((6, 2, own_lines, GRID, LANES), jnp.float32),
            pltpu.VMEM((6, 2, own_lines, GRID, LANES), jnp.float32),
            pltpu.VMEM((6, 2, ROUGH, rows, LANES), jnp.float32),
            pltpu.VMEM((2 * GRID, 6 * LANES), jnp.float32),
            pltpu.VMEM((STATS, 8, LANES), jnp.float32),
            pltpu.VMEM((slabs, STATS, LANES), jnp.float32),
            pltpu.VMEM((points, STATS, LANES), jnp.float32),
            pltpu.SemaphoreType.DMA((8,)),
            pltpu.SemaphoreType.DMA((2, rows // 8, slabs - 1, own_lines)),
            pltpu.SemaphoreType.DMA((2, rows // 8, slabs - 1, own_lines)),
            pltpu.SemaphoreType.DMA((slabs - 1,)),
            pltpu.SemaphoreType.DMA((slabs - 1,)),
            pltpu.SemaphoreType.DMA((points - 1,)),
            pltpu.SemaphoreType.DMA((points - 1,)),
        ],
        compiler_params=pltpu.CompilerParams(
            collective_id=0, has_side_effects=True, vmem_limit_bytes=60 * 1024 * 1024
        ),
    )(
        macro_strain,
        phase_ids,
        yield_flags[0],
        plastic_strain[0],
        jnp.asarray(np.stack([host_halves(depth), host_halves(depth_back)])),
        jnp.asarray(np.stack([host_halves(line), host_halves(line_back)])),
        twiddle_table().reshape(2 * ROUGH, LANES),
    )
    means = stats[:, :, 0] / float(GRID**3)
    mean_stress = means[:, :6]
    pair_place = np.zeros((6, 6), np.int32)
    place = 7
    for a in range(6):
        for b in range(a, 6):
            pair_place[a, b] = pair_place[b, a] = place
            place += 1
    outer = jnp.stack([means[:, place] for place in pair_place.reshape(-1)], axis=1)
    outer = outer.reshape(points, 6, 6)
    tangent = jax.vmap(tangent_matrix)(means[:, 6], outer)
    weights = np.asarray(PAIR_WEIGHTS)
    weighted = lookup * weights[None, :, None] * QUADRATURE_WEIGHT
    weighted = jnp.asarray(weighted.reshape(48, 24), jnp.float32)
    element_force = jnp.sum(
        mean_stress.reshape(element_count, 48, 1) * weighted[None], axis=1
    )
    best = lax.Precision.HIGHEST
    spread = jnp.einsum(
        "equn,qnv->equv",
        tangent.reshape(element_count, 8, 6, 6),
        jnp.asarray(lookup, jnp.float32),
        precision=best,
    ).reshape(element_count, 48, 24)
    element_stiffness = jnp.einsum("rh,erv->ehv", weighted, spread, precision=best)
    forces = jnp.einsum(
        "eck,ecn->nk", element_force.reshape(element_count, 8, 3), placing, precision=best
    )
    block = element_stiffness.reshape(element_count, 8, 3, 8, 3)
    stiffness = jnp.einsum("ecn,eckdl,edm->nkml", placing, block, placing, precision=best)
    stiffness = stiffness.reshape(3 * node_count, 3 * node_count)
    own_stress = lax.dynamic_slice(mean_stress, (point, 0), (1, 6))
    own_tangent = lax.dynamic_slice(tangent, (point, 0, 0), (1, 6, 6))
    return (own_stress, own_tangent, forces, stiffness)


def solution(mesh):
    slabs = mesh.shape["slab"]
    fits = slabs > 1 and ROUGH % slabs == 0 and GRID // slabs % 16 == 0
    body = fused_on_device if fits else on_device
    return jax.shard_map(
        body,
        mesh=mesh,
        in_specs=(
            P("slab", None),
            P("rve", None, "slab", None),
            P("rve", None, "slab", None),
            P(),
            P(),
        ),
        out_specs=(P("rve", None), P("rve", None, None), P(), P()),
        check_vma=False,
    )
```

```python
import math

import jax
import jax.numpy as jnp
import numpy as np
from jax import lax
from jax.experimental import pallas as pl
from jax.experimental.pallas import tpu as pltpu
from jax.sharding import PartitionSpec as P

GRID = 64
ITERS = 2


SHEAR_MODULUS = 80.0
BULK_MODULUS = 160.0
REFERENCE_SHEAR = 80.0
REFERENCE_LAME = 160.0 - 160.0 / 3.0
TANGENT_UNIT = 100.0
QUADRATURE_WEIGHT = 0.125
DIAGONAL_PART = (1.0, 1.0, 1.0, 0.0, 0.0, 0.0)
PAIR_WEIGHTS = (1.0, 1.0, 1.0, 2.0, 2.0, 2.0)
TENSOR_PAIRS = ((0, 0), (1, 1), (2, 2), (1, 2), (0, 2), (0, 1))
TENSOR_ROWS = ((0, 5, 4), (5, 1, 3), (4, 3, 2))


def gradient_table():
    inverse_root = 1.0 / math.sqrt(3.0)
    table_rows = np.zeros((8, 6, 24))
    for gauss_corner in range(8):
        position = [
            0.5 + (2 * (gauss_corner >> axis_number & 1) - 1) * 0.5 * inverse_root
            for axis_number in range(3)
        ]
        for corner in range(8):
            corner_bits = [corner >> axis_number & 1 for axis_number in range(3)]
            factors = [
                position[axis_number] * corner_bits[axis_number]
                + (1.0 - position[axis_number]) * (1 - corner_bits[axis_number])
                for axis_number in range(3)
            ]
            slopes = []
            for axis_number in range(3):
                slope_value = 2.0 * corner_bits[axis_number] - 1.0
                for other_axis in range(3):
                    if other_axis != axis_number:
                        slope_value = slope_value * factors[other_axis]
                slopes.append(slope_value)
            column = 3 * corner
            table_rows[gauss_corner, 0, column] += slopes[0]
            table_rows[gauss_corner, 1, column + 1] += slopes[1]
            table_rows[gauss_corner, 2, column + 2] += slopes[2]
            table_rows[gauss_corner, 3, column + 1] += 0.5 * slopes[2]
            table_rows[gauss_corner, 3, column + 2] += 0.5 * slopes[1]
            table_rows[gauss_corner, 4, column] += 0.5 * slopes[2]
            table_rows[gauss_corner, 4, column + 2] += 0.5 * slopes[0]
            table_rows[gauss_corner, 5, column] += 0.5 * slopes[1]
            table_rows[gauss_corner, 5, column + 1] += 0.5 * slopes[0]
    return table_rows


def point_geometry(points, connectivity, corner_lookup, node_count):
    element_count = connectivity.shape[0]
    point_count = points.shape[0]
    corner_selector = (points[:, None] % 8 == jnp.arange(8, dtype=jnp.int32)[None, :]).astype(
        jnp.float32
    )
    strain_row_values = jnp.einsum(
        "zu,utf->ztf", corner_selector, corner_lookup, precision=lax.Precision.HIGHEST
    )
    element_onehot = points[:, None] // 8 == jnp.arange(element_count, dtype=jnp.int32)[None, :]
    corner_nodes = jnp.sum(
        jnp.where(element_onehot[:, :, None], connectivity[None, :, :], 0), axis=1
    )
    degrees = 3 * corner_nodes[:, :, None] + jnp.arange(3, dtype=jnp.int32)[None, None, :]
    degrees = degrees.reshape(point_count, 24)
    placing = (
        degrees[:, :, None] == jnp.arange(3 * node_count, dtype=jnp.int32)[None, None, :]
    ).astype(jnp.float32)
    return (strain_row_values, placing)


def macro_strains(strain_row_values, placing, displacements):
    nodal_quantities = jnp.einsum(
        "gpn,n->gp", placing, displacements.reshape(-1), precision=lax.Precision.HIGHEST
    )
    return jnp.einsum(
        "vxw,vw->vx", strain_row_values, nodal_quantities, precision=lax.Precision.HIGHEST
    )


def material_response(strain, plastic, phase_ids, flag_values):
    diagonal = jnp.asarray(DIAGONAL_PART, jnp.float32)[:, None]
    weights = jnp.asarray(PAIR_WEIGHTS, jnp.float32)[:, None]
    martensite = phase_ids == 1
    yield_stress = jnp.where(martensite, 1.2, 0.3).astype(jnp.float32)
    hardening = jnp.where(martensite, 10.0, 2.0).astype(jnp.float32)
    elastic = strain - plastic
    volume = elastic[0] + elastic[1] + elastic[2]
    trial_dev = 2.0 * SHEAR_MODULUS * (elastic - diagonal * (volume / 3.0))
    equivalent = jnp.sqrt(1.5 * jnp.sum(weights * trial_dev * trial_dev, axis=0))
    bounded = jnp.maximum(equivalent, yield_stress)
    return_ratio = 3.0 * SHEAR_MODULUS / (3.0 * SHEAR_MODULUS + hardening)
    active = flag_values.astype(jnp.float32)
    plastic_flow = active * (equivalent - yield_stress) / bounded
    softening = 1.0 - return_ratio * plastic_flow
    stress = trial_dev * softening + diagonal * (BULK_MODULUS * volume)
    shear_term = 2.0 * SHEAR_MODULUS * softening
    tangent_weight = (
        3.0 * SHEAR_MODULUS * return_ratio * active * yield_stress / (bounded * bounded * bounded)
    )
    return (stress, trial_dev, shear_term, tangent_weight)


def wave_terms(index_x, index_y, index_z):
    middle = GRID // 2
    signed = []
    for indices in (index_x, index_y, index_z):
        wrapped = jnp.where(indices < middle, indices, indices - GRID)
        signed.append(jnp.where(indices == middle, 0, wrapped))
    nyquist_free = (index_x != middle) & (index_y != middle) & (index_z != middle)
    length = signed[0] * signed[0] + signed[1] * signed[1] + signed[2] * signed[2]
    keep_mask = (nyquist_free & (length > 0)).astype(jnp.float32)
    inverse_length = 1.0 / jnp.sqrt(jnp.maximum(length, 1).astype(jnp.float32))
    normals = [signed_entry.astype(jnp.float32) * inverse_length for signed_entry in signed]
    return (normals, keep_mask)


def project_green(components, normals, keep_mask):
    traction = [
        components[tensor_row[0]] * normals[0]
        + components[tensor_row[1]] * normals[1]
        + components[tensor_row[2]] * normals[2]
        for tensor_row in TENSOR_ROWS
    ]
    normal_load = normals[0] * traction[0] + normals[1] * traction[1] + normals[2] * traction[2]
    coupling = (REFERENCE_LAME + REFERENCE_SHEAR) / (
        REFERENCE_SHEAR * (REFERENCE_LAME + 2.0 * REFERENCE_SHEAR)
    )
    result_list = []
    for left_axis, right_axis in TENSOR_PAIRS:
        entry_value = (
            normals[left_axis] * traction[right_axis] + normals[right_axis] * traction[left_axis]
        ) / (2.0 * REFERENCE_SHEAR)
        entry_value = (
            entry_value - coupling * normals[left_axis] * normals[right_axis] * normal_load
        )
        result_list.append(entry_value * keep_mask)
    return jnp.stack(result_list)


def tangent_matrix(mean_shear, outer_sum):
    diagonal = jnp.asarray(DIAGONAL_PART, jnp.float32)
    volumetric = diagonal[:, None] * diagonal[None, :]
    weights = jnp.asarray(PAIR_WEIGHTS, jnp.float32)
    identity = jnp.eye(6, dtype=jnp.float32)
    whole = (
        BULK_MODULUS * volumetric
        + mean_shear * (identity - volumetric / 3.0)
        - outer_sum * weights[None, :]
    )
    return whole / TANGENT_UNIT


def assemble(stress_values, tangent_moduli, strain_row_values, placing):
    weights = jnp.asarray(PAIR_WEIGHTS, jnp.float32)
    force_row_values = strain_row_values * weights[None, :, None]
    element_force_vector = QUADRATURE_WEIGHT * jnp.einsum(
        "mbh,mb->mh", force_row_values, stress_values, precision=lax.Precision.HIGHEST
    )
    element_stiffness_matrix = QUADRATURE_WEIGHT * jnp.einsum(
        "xoh,xon,xnv->xhv",
        force_row_values,
        tangent_moduli,
        strain_row_values,
        precision=lax.Precision.HIGHEST,
    )
    forces = jnp.einsum("gp,gpn->n", element_force_vector, placing, precision=lax.Precision.HIGHEST)
    stiffness = jnp.einsum(
        "gpq,gpm,gqn->mn",
        element_stiffness_matrix,
        placing,
        placing,
        precision=lax.Precision.HIGHEST,
    )
    return (forces.reshape(-1, 3), stiffness)


def angle_table(count_rows, count_cols):
    rows_index = lax.broadcasted_iota(jnp.int32, (count_rows, count_cols), 0)
    cols_index = lax.broadcasted_iota(jnp.int32, (count_rows, count_cols), 1)
    angles = 2.0 * math.pi / GRID * (rows_index * cols_index % GRID).astype(jnp.float32)
    return (jnp.cos(angles), jnp.sin(angles))


def complex_table(inverse):
    cosine, sine = angle_table(GRID, GRID)
    if inverse:
        first_row = jnp.stack([cosine, -sine], axis=1)
        second_row = jnp.stack([sine, cosine], axis=1)
    else:
        first_row = jnp.stack([cosine, sine], axis=1)
        second_row = jnp.stack([-sine, cosine], axis=1)
    return jnp.stack([first_row, second_row], axis=0)


def on_device(phase_ids, yield_flags, plastic_strain, displacements, connectivity):
    slabs = lax.axis_size("slab")
    slab_index = lax.axis_index("slab")
    plane_count = phase_ids.shape[0]
    row_planes = GRID // slabs
    node_count = displacements.shape[0]
    corner_lookup = jnp.asarray(gradient_table(), jnp.float32)
    gauss_point = lax.axis_index("rve")
    own_points = jnp.full((1,), gauss_point, jnp.int32)
    strain_row_values, placing = point_geometry(own_points, connectivity, corner_lookup, node_count)
    macro_strain = macro_strains(strain_row_values, placing, displacements)[0]
    phases = phase_ids.reshape(-1)
    plastic = plastic_strain[0].reshape(6, -1)
    point_flags = yield_flags[0]
    columns = GRID // 2
    kept_index = lax.broadcasted_iota(jnp.int32, (columns, 1), 0)
    column_weight = jnp.where(kept_index == 0, 1.0, 2.0).astype(jnp.float32)
    depth_cos, depth_sin = angle_table(columns, GRID)
    forward_depth = jnp.stack([depth_cos, -depth_sin], axis=0)
    inverse_depth = jnp.stack(
        [column_weight * depth_cos, -column_weight * depth_sin], axis=0
    ) / float(GRID**3)
    forward_plane = complex_table(False)
    inverse_plane = complex_table(True)
    index_x = lax.broadcasted_iota(jnp.int32, (GRID, 1, 1), 0)
    index_y = slab_index * row_planes + lax.broadcasted_iota(jnp.int32, (1, row_planes, 1), 1)
    index_z = lax.broadcasted_iota(jnp.int32, (1, 1, columns), 2)
    normals, keep_mask = wave_terms(index_x, index_y, index_z)
    strain = jnp.broadcast_to(macro_strain[:, None], plastic.shape)
    for iteration in range(ITERS):
        stress = material_response(strain, plastic, phases, point_flags[iteration].reshape(-1))[0]
        voxel_block = stress.reshape(6, plane_count, GRID, GRID)
        spectral = jnp.einsum(
            "pkz,cxyz->pcxyk", forward_depth, voxel_block, precision=lax.Precision.HIGHEST
        )
        spectral = jnp.einsum(
            "pjqy,qcxyk->pcxjk", forward_plane, spectral, precision=lax.Precision.HIGHEST
        )
        spectral = lax.all_to_all(spectral, "slab", split_axis=3, concat_axis=2, tiled=True)
        spectral = jnp.einsum(
            "pjqx,qcxyk->pcjyk", forward_plane, spectral, precision=lax.Precision.HIGHEST
        )
        projected = project_green(
            [spectral[:, component] for component in range(6)], normals, keep_mask
        )
        spectral = jnp.einsum(
            "pjqx,cqxyk->pcjyk", inverse_plane, projected, precision=lax.Precision.HIGHEST
        )
        spectral = lax.all_to_all(spectral, "slab", split_axis=2, concat_axis=3, tiled=True)
        spectral = jnp.einsum(
            "pjqy,qcxyk->pcxjk", inverse_plane, spectral, precision=lax.Precision.HIGHEST
        )
        correction = jnp.einsum(
            "pkz,pcxyk->cxyz", inverse_depth, spectral, precision=lax.Precision.HIGHEST
        )
        strain = strain - correction.reshape(6, -1)
    stress, trial_dev, shear_term, tangent_weight = material_response(
        strain, plastic, phases, point_flags[ITERS].reshape(-1)
    )
    outer_part = jnp.dot(
        trial_dev * tangent_weight[None, :], trial_dev.T, precision=lax.Precision.HIGHEST
    )
    stress_total, shear_total, outer_total = lax.psum(
        (jnp.sum(stress, axis=1), jnp.sum(shear_term), outer_part), "slab"
    )
    voxel_count = float(GRID**3)
    mean_stress = stress_total / voxel_count
    tangent = tangent_matrix(shear_total / voxel_count, outer_total / voxel_count)
    own_forces, own_stiffness = assemble(
        mean_stress[None], tangent[None], strain_row_values, placing
    )
    forces, stiffness = lax.psum((own_forces, own_stiffness), "rve")
    return (mean_stress[None], tangent[None], forces, stiffness)


ROUGH = 16
GROUPS = 4
LANES = 128
STATS = 32
MESH = pl.DeviceIdType.MESH


def halves(value):
    high = value.astype(jnp.bfloat16)
    return high, (value - high.astype(jnp.float32)).astype(jnp.bfloat16)


def mul(left, right):
    return jnp.dot(left, right, preferred_element_type=jnp.float32)


def host_halves(table):
    table = np.asarray(table, np.float32)
    high = table.astype(jnp.bfloat16)
    low = (table - high.astype(np.float32)).astype(jnp.bfloat16)
    return np.stack([high, low])


def depth_tables():
    kept = GRID // 2
    angles = 2.0 * np.pi / GRID * (np.arange(GRID)[:, None] * np.arange(kept)[None, :] % GRID)
    weight = np.where(np.arange(kept) == 0, 1.0, 2.0) / float(GRID**3)
    eye = np.eye(GROUPS)
    forward = np.concatenate([np.kron(eye, np.cos(angles)), np.kron(eye, -np.sin(angles))], axis=1)
    back_cos = (np.cos(angles) * weight[None, :]).T
    back_sin = (-np.sin(angles) * weight[None, :]).T
    inverse = np.concatenate([np.kron(eye, back_cos), np.kron(eye, back_sin)], axis=0)
    return forward, inverse


def line_tables():
    angles = 2.0 * np.pi / GRID * (np.arange(GRID)[:, None] * np.arange(GRID)[None, :] % GRID)
    cosine, sine = np.cos(angles), np.sin(angles)
    forward = np.block([[cosine, sine], [-sine, cosine]])
    inverse = np.block([[cosine, -sine], [sine, cosine]])
    return forward, inverse


def twiddle_table():
    lane_group = np.arange(LANES) // (LANES // GROUPS)
    angles = 2.0 * np.pi / GRID * (np.arange(ROUGH)[:, None] * lane_group[None, :])
    return jnp.asarray(np.stack([np.cos(angles), -np.sin(angles)], axis=1), jnp.float32)


def four_point(re, im, sign):
    a_re, a_im = re[0] + re[2], im[0] + im[2]
    b_re, b_im = re[0] - re[2], im[0] - im[2]
    c_re, c_im = re[1] + re[3], im[1] + im[3]
    d_re, d_im = re[1] - re[3], im[1] - im[3]
    e_re, e_im = (d_im, -d_re) if sign < 0 else (-d_im, d_re)
    return (
        [a_re + c_re, b_re + e_re, a_re - c_re, b_re - e_re],
        [a_im + c_im, b_im + e_im, a_im - c_im, b_im - e_im],
    )


def sixteen_point(re, im, sign):
    inner_re, inner_im = [], []
    for b in range(4):
        part_re, part_im = four_point(re[b::4], im[b::4], sign)
        for ka in range(1, 4):
            if b:
                angle = 2.0 * math.pi * b * ka / 16.0
                cosine, sine = math.cos(angle), sign * math.sin(angle)
                old_re, old_im = part_re[ka], part_im[ka]
                part_re[ka] = old_re * cosine - old_im * sine
                part_im[ka] = old_re * sine + old_im * cosine
        inner_re.append(part_re)
        inner_im.append(part_im)
    out_re, out_im = [None] * 16, [None] * 16
    for ka in range(4):
        part_re, part_im = four_point(
            [inner_re[b][ka] for b in range(4)], [inner_im[b][ka] for b in range(4)], sign
        )
        for kb in range(4):
            out_re[ka + 4 * kb] = part_re[kb]
            out_im[ka + 4 * kb] = part_im[kb]
    return out_re, out_im


def voxel_law(elastic, phase, flag, want_tangent):
    martensite = phase == 1
    yield_stress = jnp.where(martensite, 1.2, 0.3).astype(jnp.float32)
    base = 3.0 * SHEAR_MODULUS
    ratio = jnp.where(martensite, base / (base + 10.0), base / (base + 2.0)).astype(jnp.float32)
    volume = elastic[0] + elastic[1] + elastic[2]
    third = volume * (1.0 / 3.0)
    trial = [
        (2.0 * SHEAR_MODULUS) * (elastic[n] - third if n < 3 else elastic[n]) for n in range(6)
    ]
    square = [value * value for value in trial]
    norm = square[0] + square[1] + square[2] + 2.0 * (square[3] + square[4] + square[5])
    equivalent = jnp.sqrt(1.5 * norm)
    bounded = jnp.maximum(equivalent, yield_stress)
    active = flag.astype(jnp.float32)
    inverse = 1.0 / bounded
    active_ratio = active * ratio
    softening = 1.0 - active_ratio * ((equivalent - yield_stress) * inverse)
    pressure = BULK_MODULUS * volume
    stress = [trial[n] * softening + pressure if n < 3 else trial[n] * softening for n in range(6)]
    if not want_tangent:
        return stress
    beta = base * active_ratio * yield_stress * (inverse * inverse * inverse)
    return stress, trial, (2.0 * SHEAR_MODULUS) * softening, beta


def cell_kernel(
    slabs, points, macro_ref, phase_hbm, flag_hbm, plastic_hbm, depth_hbm, line_hbm, twiddle_hbm,
    out_ref,
    phase_ref, flag_ref, depth_ref, line_ref, twiddle_ref,
    elastic, planes, lines, lines_back, planes_back, work, sums, slab_sums, point_sums,
    load_sem, send_sem, recv_sem, slab_send, slab_recv, point_send, point_recv,
):
    slab = lax.axis_index("slab")
    point = lax.axis_index("rve")
    rows = GRID // slabs
    own_lines = ROUGH // slabs
    wide = GROUPS * GRID

    barrier = pltpu.get_barrier_semaphore()
    for step in range(1, slabs):
        pl.semaphore_signal(
            barrier, inc=1, device_id={"slab": lax.rem(slab + step, slabs)}, device_id_type=MESH
        )
    for step in range(1, points):
        pl.semaphore_signal(
            barrier, inc=1, device_id={"rve": lax.rem(point + step, points)}, device_id_type=MESH
        )

    def lane_block(index):
        return pl.ds(pl.multiple_of(index * wide, wide), wide)

    def row_block(index):
        return pl.ds(pl.multiple_of(index * rows, rows), rows)

    parts = rows // 8

    def part_rows(part):
        return pl.ds(pl.multiple_of(part * 8, 8), 8)

    pairs = [
        (plastic_hbm.at[:, 0:8], elastic.at[:, 0:8]),
        (phase_hbm, phase_ref),
        (flag_hbm.at[0], flag_ref.at[0]),
        (depth_hbm, depth_ref),
        (twiddle_hbm, twiddle_ref),
        (plastic_hbm.at[:, 8:rows], elastic.at[:, 8:rows]),
        (line_hbm, line_ref),
        (flag_hbm.at[1:], flag_ref.at[1:]),
    ]
    loads = [
        pltpu.make_async_copy(source, target, load_sem.at[place])
        for place, (source, target) in enumerate(pairs)
    ]
    for load in loads:
        load.start()

    lane = lax.broadcasted_iota(jnp.int32, (1, LANES), 1)
    group = lane >> 5
    high_sign = jnp.where((group >> 1) == 0, 1.0, -1.0).astype(jnp.float32)
    low_sign = jnp.where((group & 1) == 0, 1.0, -1.0).astype(jnp.float32)
    low_first = (group & 1) == 0
    corner = group == 3

    def across_high(value):
        return pltpu.roll(value, 64, 1) + high_sign * value

    def across_low(value):
        partner = jnp.where(low_first, pltpu.roll(value, 96, 1), pltpu.roll(value, 32, 1))
        return partner + low_sign * value

    def groups_forward(re, im, cosine, sine):
        re, im = re * cosine - im * sine, re * sine + im * cosine
        re, im = across_high(re), across_high(im)
        re, im = jnp.where(corner, im, re), jnp.where(corner, -re, im)
        return across_low(re), across_low(im)

    def groups_back(re, im, cosine, sine):
        re, im = across_low(re), across_low(im)
        re, im = jnp.where(corner, -im, re), jnp.where(corner, re, im)
        re, im = across_high(re), across_high(im)
        return re * cosine + im * sine, im * cosine - re * sine

    def sixteen(ref, sign, part):
        @pl.loop(0, 6)
        def _(n):
            picked = part_rows(part)
            re = [ref[n, 0, k, picked, :] for k in range(ROUGH)]
            im = [ref[n, 1, k, picked, :] for k in range(ROUGH)]
            re, im = sixteen_point(re, im, sign)
            for k in range(ROUGH):
                ref[n, 0, k, picked, :] = re[k]
                ref[n, 1, k, picked, :] = im[k]

    def slab_rows(index, part):
        return pl.ds(pl.multiple_of(index * rows + part * 8, 8), 8)

    def forward_copy(step, chunk, part, target, source):
        return pltpu.make_async_remote_copy(
            src_ref=planes.at[:, :, target * own_lines + chunk, part_rows(part), :],
            dst_ref=lines.at[:, :, chunk, slab_rows(source, part), :],
            send_sem=send_sem.at[0, part, step - 1, chunk],
            recv_sem=recv_sem.at[0, part, step - 1, chunk],
            device_id={"slab": target},
            device_id_type=MESH,
        )

    def back_copy(step, chunk, part, target, source):
        return pltpu.make_async_remote_copy(
            src_ref=lines_back.at[:, :, chunk, slab_rows(target, part), :],
            dst_ref=planes_back.at[:, :, source * own_lines + chunk, part_rows(part), :],
            send_sem=send_sem.at[1, part, step - 1, chunk],
            recv_sem=recv_sem.at[1, part, step - 1, chunk],
            device_id={"slab": target},
            device_id_type=MESH,
        )

    def to(step):
        return lax.rem(slab + step, slabs)

    def come_from(step):
        return lax.rem(slab + slabs - step, slabs)

    coupling = (REFERENCE_LAME + REFERENCE_SHEAR) / (
        REFERENCE_SHEAR * (REFERENCE_LAME + 2.0 * REFERENCE_SHEAR)
    )
    middle = GRID // 2

    def signed(index):
        wrapped = jnp.where(index < middle, index, index - GRID)
        return jnp.where(index == middle, 0, wrapped)

    def line_stage(chunk):
        stacked = jnp.concatenate(
            [lines[n, :, chunk].reshape(2 * GRID, LANES) for n in range(6)], axis=1
        )
        high, low = halves(stacked)
        work[...] = mul(line_ref[0, 0], high) + mul(line_ref[0, 0], low) + mul(line_ref[0, 1], high)
        index_y = slab * own_lines + chunk + ROUGH * ((group >> 1) + 2 * (group & 1))
        index_z = lane & (LANES // GROUPS - 1)
        freq_y = signed(index_y)
        freq_z = index_z

        @pl.loop(0, GRID // 8)
        def _(block):
            index_x = block * 8 + lax.broadcasted_iota(jnp.int32, (8, 1), 0)
            freq_x = signed(index_x)
            length = freq_x * freq_x + (freq_y * freq_y + freq_z * freq_z)
            keep = (index_x != middle) & (index_y != middle) & (length > 0)
            inverse = jnp.where(keep, 1.0 / jnp.maximum(length, 1).astype(jnp.float32), 0.0)
            scale = inverse * (1.0 / REFERENCE_SHEAR)
            along = coupling * inverse * inverse
            xi = [freq.astype(jnp.float32) for freq in (freq_x, freq_y, freq_z)]
            for part in range(2):
                picked = pl.ds(pl.multiple_of(part * GRID + block * 8, 8), 8)
                tau = [work[picked, n * LANES : (n + 1) * LANES] for n in range(6)]
                load = [
                    tau[row[0]] * xi[0] + tau[row[1]] * xi[1] + tau[row[2]] * xi[2]
                    for row in TENSOR_ROWS
                ]
                normal = (xi[0] * load[0] + xi[1] * load[1] + xi[2] * load[2]) * along
                field = [0.5 * (load[d] * scale - xi[d] * normal) for d in range(3)]
                for n, (left, right) in enumerate(TENSOR_PAIRS):
                    value = xi[left] * field[right] + xi[right] * field[left]
                    work[picked, n * LANES : (n + 1) * LANES] = value

        high, low = halves(work[...])
        result = (
            mul(line_ref[1, 0], high) + mul(line_ref[1, 0], low) + mul(line_ref[1, 1], high)
        )
        for n in range(6):
            lines_back[n, :, chunk] = result[:, n * LANES : (n + 1) * LANES].reshape(
                2, GRID, LANES
            )

    def twiddles(line):
        return twiddle_ref[pl.ds(2 * line, 1), :], twiddle_ref[pl.ds(2 * line + 1, 1), :]

    def plane_forward(iteration, part):
        picked = part_rows(part)

        @pl.loop(0, ROUGH // 8)
        def _(batch):
            pieces = []
            for inner in range(8):
                at = lane_block(batch * 8 + inner)
                pieces += voxel_law(
                    [elastic[n, picked, at] for n in range(6)],
                    phase_ref[picked, at],
                    flag_ref[iteration, picked, at],
                    False,
                )
            high, low = halves(jnp.concatenate(pieces, axis=0))
            result = (
                mul(high, depth_ref[0, 0]) + mul(low, depth_ref[0, 0]) + mul(high, depth_ref[0, 1])
            )
            for inner in range(8):
                for n in range(6):
                    first = (inner * 6 + n) * 8
                    planes[n, 0, batch * 8 + inner, picked, :] = result[first : first + 8, :LANES]
                    planes[n, 1, batch * 8 + inner, picked, :] = result[first : first + 8, LANES:]

        sixteen(planes, -1, part)

        @pl.loop(0, own_lines)
        def _(chunk):
            for step in list(range(1, slabs)) + [0]:
                target = to(step)
                line = target * own_lines + chunk
                cosine, sine = twiddles(line)
                for n in range(6):
                    re, im = groups_forward(
                        planes[n, 0, line, picked, :], planes[n, 1, line, picked, :], cosine, sine
                    )
                    if step:
                        planes[n, 0, line, picked, :] = re
                        planes[n, 1, line, picked, :] = im
                    else:
                        lines[n, 0, chunk, slab_rows(slab, part), :] = re
                        lines[n, 1, chunk, slab_rows(slab, part), :] = im
                if step:
                    forward_copy(step, chunk, part, target, slab).start()

    def plane_back(part):
        picked = part_rows(part)

        @pl.loop(0, own_lines)
        def _(chunk):
            for step in range(slabs):
                source = come_from(step)
                line = source * own_lines + chunk
                if step:
                    back_copy(step, chunk, part, to(step), source).wait_recv()
                cosine, sine = twiddles(line)
                for n in range(6):
                    if step:
                        re = planes_back[n, 0, line, picked, :]
                        im = planes_back[n, 1, line, picked, :]
                    else:
                        re = lines_back[n, 0, chunk, slab_rows(slab, part), :]
                        im = lines_back[n, 1, chunk, slab_rows(slab, part), :]
                    re, im = groups_back(re, im, cosine, sine)
                    planes_back[n, 0, line, picked, :] = re
                    planes_back[n, 1, line, picked, :] = im

        sixteen(planes_back, 1, part)

        @pl.loop(0, ROUGH // 8)
        def _(batch):
            stacked = jnp.concatenate(
                [
                    jnp.concatenate(
                        [
                            planes_back[n, side, batch * 8 + inner, picked, :]
                            for inner in range(8)
                            for n in range(6)
                        ],
                        axis=0,
                    )
                    for side in range(2)
                ],
                axis=1,
            )
            high, low = halves(stacked)
            result = (
                mul(high, depth_ref[1, 0]) + mul(low, depth_ref[1, 0]) + mul(high, depth_ref[1, 1])
            )
            for inner in range(8):
                at = lane_block(batch * 8 + inner)
                for n in range(6):
                    first = (inner * 6 + n) * 8
                    elastic[n, picked, at] = elastic[n, picked, at] - result[first : first + 8]

    def final_sums(part):
        picked = part_rows(part)

        @pl.loop(0, ROUGH)
        def _(block):
            at = lane_block(block)
            stress, trial, shear, beta = voxel_law(
                [elastic[n, picked, at] for n in range(6)],
                phase_ref[picked, at],
                flag_ref[ITERS, picked, at],
                True,
            )
            entries = stress + [shear]
            for a in range(6):
                weighted = beta * trial[a]
                for b in range(a, 6):
                    entries.append(weighted * trial[b])
            for place, value in enumerate(entries):
                sums[place] = sums[place] + (value[:, :LANES] + value[:, LANES:])

    sums[...] = jnp.zeros_like(sums)
    for load in loads[:5]:
        load.wait()

    @pl.loop(0, parts)
    def _(part):
        @pl.when(part == 1)
        def _():
            loads[5].wait()

        picked = part_rows(part)

        @pl.loop(0, ROUGH)
        def _(block):
            at = lane_block(block)
            for n in range(6):
                elastic[n, picked, at] = macro_ref[n] - elastic[n, picked, at]

        @pl.when(part == 0)
        def _():
            pl.semaphore_wait(barrier, slabs - 1 + points - 1)

        plane_forward(0, part)

    for load in loads[6:]:
        load.wait()

    @pl.loop(0, ITERS)
    def _(iteration):
        @pl.loop(0, own_lines)
        def _(chunk):
            for step in range(1, slabs):
                for part in range(parts):
                    forward_copy(step, chunk, part, to(step), come_from(step)).wait_recv()
            line_stage(chunk)
            for step in range(1, slabs):
                back_copy(step, chunk, 0, to(step), slab).start()

        @pl.loop(0, own_lines)
        def _(chunk):
            for part in range(1, parts):
                for step in range(1, slabs):
                    back_copy(step, chunk, part, to(step), slab).start()

        @pl.loop(0, parts)
        def _(part):
            plane_back(part)

            @pl.loop(0, own_lines)
            def _(chunk):
                for step in range(1, slabs):
                    forward_copy(step, chunk, part, to(step), slab).wait_send()
                    back_copy(step, chunk, part, to(step), slab).wait_send()

            @pl.when(iteration < ITERS - 1)
            def _():
                plane_forward(iteration + 1, part)

            @pl.when(iteration == ITERS - 1)
            def _():
                final_sums(part)

    slab_sums[slab] = jnp.sum(sums[...], axis=1)

    def slab_copy(step, source):
        return pltpu.make_async_remote_copy(
            src_ref=slab_sums.at[source],
            dst_ref=slab_sums.at[source],
            send_sem=slab_send.at[step - 1],
            recv_sem=slab_recv.at[step - 1],
            device_id={"slab": to(step)},
            device_id_type=MESH,
        )

    def point_copy(step, source):
        return pltpu.make_async_remote_copy(
            src_ref=point_sums.at[source],
            dst_ref=point_sums.at[source],
            send_sem=point_send.at[step - 1],
            recv_sem=point_recv.at[step - 1],
            device_id={"rve": lax.rem(point + step, points)},
            device_id_type=MESH,
        )

    for step in range(1, slabs):
        slab_copy(step, slab).start()
    for step in range(1, slabs):
        slab_copy(step, come_from(step)).wait_recv()
    total = slab_sums[0]
    for other in range(1, slabs):
        total = total + slab_sums[other]
    point_sums[point] = jnp.broadcast_to(
        jnp.sum(total, axis=1, keepdims=True), (STATS, LANES)
    )
    for step in range(1, points):
        point_copy(step, point).start()
    for step in range(1, points):
        point_copy(step, lax.rem(point + points - step, points)).wait_recv()
    out_ref[...] = point_sums[...]
    for step in range(1, slabs):
        slab_copy(step, slab).wait_send()
    for step in range(1, points):
        point_copy(step, point).wait_send()


def fused_on_device(phase_ids, yield_flags, plastic_strain, displacements, connectivity):
    slabs = lax.axis_size("slab")
    points = lax.axis_size("rve")
    rows = phase_ids.shape[0]
    node_count = displacements.shape[0]
    element_count = connectivity.shape[0]
    own_lines = ROUGH // slabs
    point = lax.axis_index("rve")
    lookup = gradient_table()
    placing = (
        connectivity[:, :, None] == jnp.arange(node_count, dtype=jnp.int32)[None, None, :]
    ).astype(jnp.float32)
    corner_moves = jnp.sum(placing[:, :, :, None] * displacements[None, None, :, :], axis=2)
    all_strain = jnp.sum(
        jnp.asarray(lookup, jnp.float32)[None] * corner_moves.reshape(element_count, 1, 1, 24),
        axis=3,
    ).reshape(points, 6)
    macro_strain = lax.dynamic_slice(all_strain, (point, 0), (1, 6))[0]

    depth, depth_back = depth_tables()
    line, line_back = line_tables()
    wide = GROUPS * GRID
    vmem = pl.BlockSpec(memory_space=pltpu.VMEM)
    stats = pl.pallas_call(
        lambda *refs: cell_kernel(slabs, points, *refs),
        out_shape=jax.ShapeDtypeStruct((points, STATS, LANES), jnp.float32),
        in_specs=[pl.BlockSpec(memory_space=pltpu.SMEM)]
        + [pl.BlockSpec(memory_space=pltpu.HBM)] * 6,
        out_specs=vmem,
        scratch_shapes=[
            pltpu.VMEM((rows, GRID * GRID), jnp.int32),
            pltpu.VMEM((ITERS + 1, rows, GRID * GRID), jnp.int32),
            pltpu.VMEM((2, 2, wide, wide), jnp.bfloat16),
            pltpu.VMEM((2, 2, 2 * GRID, 2 * GRID), jnp.bfloat16),
            pltpu.VMEM((2 * ROUGH, LANES), jnp.float32),
            pltpu.VMEM((6, rows, GRID * GRID), jnp.float32),
            pltpu.VMEM((6, 2, ROUGH, rows, LANES), jnp.float32),
            pltpu.VMEM((6, 2, own_lines, GRID, LANES), jnp.float32),
            pltpu.VMEM((6, 2, own_lines, GRID, LANES), jnp.float32),
            pltpu.VMEM((6, 2, ROUGH, rows, LANES), jnp.float32),
            pltpu.VMEM((2 * GRID, 6 * LANES), jnp.float32),
            pltpu.VMEM((STATS, 8, LANES), jnp.float32),
            pltpu.VMEM((slabs, STATS, LANES), jnp.float32),
            pltpu.VMEM((points, STATS, LANES), jnp.float32),
            pltpu.SemaphoreType.DMA((8,)),
            pltpu.SemaphoreType.DMA((2, rows // 8, slabs - 1, own_lines)),
            pltpu.SemaphoreType.DMA((2, rows // 8, slabs - 1, own_lines)),
            pltpu.SemaphoreType.DMA((slabs - 1,)),
            pltpu.SemaphoreType.DMA((slabs - 1,)),
            pltpu.SemaphoreType.DMA((points - 1,)),
            pltpu.SemaphoreType.DMA((points - 1,)),
        ],
        compiler_params=pltpu.CompilerParams(
            collective_id=0, has_side_effects=True, vmem_limit_bytes=60 * 1024 * 1024
        ),
    )(
        macro_strain,
        phase_ids,
        yield_flags[0],
        plastic_strain[0],
        jnp.asarray(np.stack([host_halves(depth), host_halves(depth_back)])),
        jnp.asarray(np.stack([host_halves(line), host_halves(line_back)])),
        twiddle_table().reshape(2 * ROUGH, LANES),
    )
    means = stats[:, :, 0] / float(GRID**3)
    mean_stress = means[:, :6]
    pair_place = np.zeros((6, 6), np.int32)
    place = 7
    for a in range(6):
        for b in range(a, 6):
            pair_place[a, b] = pair_place[b, a] = place
            place += 1
    outer = jnp.stack([means[:, place] for place in pair_place.reshape(-1)], axis=1)
    outer = outer.reshape(points, 6, 6)
    tangent = jax.vmap(tangent_matrix)(means[:, 6], outer)
    weights = np.asarray(PAIR_WEIGHTS)
    weighted = lookup * weights[None, :, None] * QUADRATURE_WEIGHT
    weighted = jnp.asarray(weighted.reshape(48, 24), jnp.float32)
    element_force = jnp.sum(
        mean_stress.reshape(element_count, 48, 1) * weighted[None], axis=1
    )
    best = lax.Precision.HIGHEST
    spread = jnp.einsum(
        "equn,qnv->equv",
        tangent.reshape(element_count, 8, 6, 6),
        jnp.asarray(lookup, jnp.float32),
        precision=best,
    ).reshape(element_count, 48, 24)
    element_stiffness = jnp.einsum("rh,erv->ehv", weighted, spread, precision=best)
    forces = jnp.einsum(
        "eck,ecn->nk", element_force.reshape(element_count, 8, 3), placing, precision=best
    )
    block = element_stiffness.reshape(element_count, 8, 3, 8, 3)
    stiffness = jnp.einsum("ecn,eckdl,edm->nkml", placing, block, placing, precision=best)
    stiffness = stiffness.reshape(3 * node_count, 3 * node_count)
    own_stress = lax.dynamic_slice(mean_stress, (point, 0), (1, 6))
    own_tangent = lax.dynamic_slice(tangent, (point, 0, 0), (1, 6, 6))
    return (own_stress, own_tangent, forces, stiffness)


def solution(mesh):
    slabs = mesh.shape["slab"]
    fits = slabs > 1 and ROUGH % slabs == 0 and GRID // slabs % 16 == 0
    body = fused_on_device if fits else on_device
    return jax.shard_map(
        body,
        mesh=mesh,
        in_specs=(
            P("slab", None),
            P("rve", None, "slab", None),
            P("rve", None, "slab", None),
            P(),
            P(),
        ),
        out_specs=(P("rve", None), P("rve", None, None), P(), P()),
        check_vma=False,
    )
```
